256 devices in a mesh: region: 16 (over z, core), chan: 16 (over x, y).
Axes of the slice: x: 4, y: 4, z: 8, core: 2. Of those that a mesh axis runs over, the one named last changes fastest.
Arguments:
- features: bfloat16 [384, 256, 256], P('chan', 'region'), may hold values from -6 to 6
- cotangent: bfloat16 [384, 256, 256], P('chan', 'region'), may hold values from -12 to 12
- neighbours: int32 [8, 256], P(None, 'region'), may hold values from 0 to 256, as said below
- kernel: float32 [384, 49], P('chan'), may hold values from -0.875 to 0.875
- norm_gain: float32 [384], replicated, may hold values from 0.25 to 1.75
- norm_shift: float32 [384], replicated, may hold values from -3 to 3
- weight_in: bfloat16 [1536, 384], replicated, may hold values from -0.3125 to 0.3125
- bias_in: float32 [1536], replicated, may hold values from -3 to 3
- weight_out: bfloat16 [384, 1536], replicated, may hold values from -0.15625 to 0.15625
- layer_scale: float32 [384], replicated, may hold values from 0.3 to 1
Outputs:
- output: bfloat16 [384, 256, 256], P('chan', 'region')
- input_grad: bfloat16 [384, 256, 256], P('chan', 'region')
- grad_weight_in: float32 [1536, 384], replicated
- grad_weight_out: float32 [384, 1536], replicated
- grad_bias_in: float32 [1536], replicated
- grad_gain: float32 [384], replicated
- grad_shift: float32 [384], replicated
- grad_scale: float32 [384], replicated
- grad_kernel: float32 [384, 49], P('chan')
The draws below stay inside these ranges and needn't reach their ends.
Inputs may be any that keep to these rules, and one draw needn't show every extreme that they name: `neighbours`: tiles are numbered row by row over the foreground cells of a slab 8 tiles across, half of whose cells are foreground. Row d holds for each tile the tile beside it in direction d (north, south, west, east, north-west, north-east, south-west, south-east), or 256 where that cell is background or outside the slab. Every neighbour lies in the tile's own block of 16 tiles or in an adjacent one.
All inputs are finite; a program needn't handle non-finite values.
Results may differ from the reference program's by a relative error of at most 0.008.
Values may be sent and summed in bfloat16 or wider, within the bound.
No kernel may reach another device: no remote copies, remote signals or barrier semaphores. Data moves between devices by JAX's collectives and lax.ppermute only.
A program may use at most 128 MiB of HBM per device.

```python
import math
import jax
import jax.numpy as jnp
from jax import lax

C = 384
HID = 1536
TS = 16
TILE_DEV = 16
TILES = 256
GC = 8
N_REGION = 16


def draw_neighbours(key, part):
    key = jax.random.fold_in(key, 11)
    cells = 2 * TILES
    grid_rows = cells // GC
    shuffled = jax.random.permutation(key, cells)
    chosen = jnp.sort(shuffled[:TILES]).astype(jnp.int32)
    inverse = jnp.full((cells,), TILES, jnp.int32).at[chosen].set(jnp.arange(TILES, dtype=jnp.int32))
    row_of = chosen // GC
    col_of = chosen % GC
    offsets = [(-1, 0), (1, 0), (0, -1), (0, 1), (-1, -1), (-1, 1), (1, -1), (1, 1)]
    result = []
    for row_step, col_step in offsets:
        new_row = row_of + row_step
        new_col = col_of + col_step
        inside = (new_row >= 0) & (new_row < grid_rows) & (new_col >= 0) & (new_col < GC)
        target = jnp.clip(new_row, 0, grid_rows - 1) * GC + jnp.clip(new_col, 0, GC - 1)
        result.append(jnp.where(inside, inverse[target], TILES))
    return jnp.stack(result).astype(jnp.int32)


def draw_cotangent(key, part):
    key = jax.random.fold_in(key, 5)
    ramp = 1.0 + 2.0 * jnp.arange(TILES, dtype=jnp.float32) / max(TILES - 1, 1)
    ramp = ramp[None, :, None]
    shape = (C, TILES, TS * TS)
    values = jax.random.truncated_normal(key, -4.0, 4.0, shape, jnp.float32) * ramp
    return values.astype(jnp.bfloat16)


def levels(own_key, dims, pieces, least, top_value):
    def one(position, blocks):
        draws = jax.random.uniform(jax.random.fold_in(jax.random.fold_in(own_key, 6), position), (blocks,), jnp.float32, least / len(pieces), top_value / len(pieces))
        return jnp.repeat(jnp.exp(draws), dims[position] // blocks).reshape((-1,) + (1,) * (len(dims) - position - 1))

    factor_of = one(*pieces[0])
    for cut in pieces[1:]:
        factor_of = factor_of * one(*cut)
    return factor_of


def scatter_about(stream_key, shape, spread, most, split=(), held_as=jnp.bfloat16):
    array = spread * jax.random.normal(stream_key, shape, jnp.float32)
    if split:
        array = array * levels(stream_key, shape, split, -0.22, 0.18)
    return jnp.clip(array, -most, most).astype(held_as)


def setup_inputs(seed: int = 0) -> dict:
    key_list = jax.random.split(jax.random.key(seed), 11)
    features = scatter_about(key_list[0], (C, TILES, TS * TS), 1.0, 6.0, ((0, 16), (1, 16)))
    cotangent = draw_cotangent(jax.random.fold_in(key_list[10], 71), 0)
    neighbours = draw_neighbours(jax.random.fold_in(key_list[10], 71), 0)
    kernel = scatter_about(key_list[3], (C, 49), 49 ** -0.5, 0.875, ((0, 16),), jnp.float32)
    norm_gain = jnp.clip(1.0 + 0.15 * jax.random.normal(key_list[4], (C,), jnp.float32), 0.25, 1.75)
    norm_shift = scatter_about(key_list[5], (C,), 0.5, 3.0, (), jnp.float32)
    weight_in = scatter_about(key_list[6], (HID, C), C ** -0.5, 0.3125)
    bias_in = scatter_about(key_list[7], (HID,), 0.5, 3.0, (), jnp.float32)
    weight_out = scatter_about(key_list[8], (C, HID), HID ** -0.5, 0.15625)
    layer_scale = jnp.clip(jnp.exp(jax.random.uniform(key_list[9], (C,), jnp.float32, math.log(0.3), math.log(1.0))), 0.3, 1.0)
    return {"features": features, "cotangent": cotangent, "neighbours": neighbours, "kernel": kernel, "norm_gain": norm_gain, "norm_shift": norm_shift, "weight_in": weight_in, "bias_in": bias_in, "weight_out": weight_out, "layer_scale": layer_scale}


def pack_rims(tiles):
    chan_count = tiles.shape[0]
    tile_count = tiles.shape[1]
    tile_side = TS
    square = tiles.reshape(chan_count, tile_count, tile_side, tile_side)
    upper = square[:, :, :3, :].reshape(chan_count, tile_count, 3 * tile_side)
    lower = square[:, :, tile_side - 3:, :].reshape(chan_count, tile_count, 3 * tile_side)
    west_cols = square[:, :, :, :3].reshape(chan_count, tile_count, 3 * tile_side)
    east_cols = square[:, :, :, tile_side - 3:].reshape(chan_count, tile_count, 3 * tile_side)
    return jnp.concatenate([upper, lower, west_cols, east_cols], axis=2)

def assemble(center, rim_table, lookup):
    chan_count = center.shape[0]
    tile_count = center.shape[1]
    tile_side = TS
    strip = 3 * tile_side

    def piece(direction):
        return jnp.take(rim_table, lookup[direction], axis=1)

    def upper_of(direction):
        return piece(direction)[:, :, :strip].reshape(chan_count, tile_count, 3, tile_side)

    def lower_of(direction):
        return piece(direction)[:, :, strip:2 * strip].reshape(chan_count, tile_count, 3, tile_side)

    def west_of(direction):
        return piece(direction)[:, :, 2 * strip:3 * strip].reshape(chan_count, tile_count, tile_side, 3)

    def east_of(direction):
        return piece(direction)[:, :, 3 * strip:].reshape(chan_count, tile_count, tile_side, 3)
    north = lower_of(0)
    south = upper_of(1)
    west = east_of(2)
    east = west_of(3)
    north_west = lower_of(4)[..., tile_side - 3:]
    north_east = lower_of(5)[..., :3]
    south_west = upper_of(6)[..., tile_side - 3:]
    south_east = upper_of(7)[..., :3]
    top_band = jnp.concatenate([north_west, north, north_east], axis=3)
    middle = jnp.concatenate([west, center.reshape(chan_count, tile_count, tile_side, tile_side), east], axis=3)
    bottom_band = jnp.concatenate([south_west, south, south_east], axis=3)
    padded = jnp.concatenate([top_band, middle, bottom_band], axis=2)
    width = tile_side + 6
    flat = padded.reshape(chan_count, tile_count, width * width)
    return jnp.pad(flat, ((0, 0), (0, 0), (0, 6)))

def depthwise(flat, weights):
    chan_count = flat.shape[0]
    tile_count = flat.shape[1]
    tile_side = TS
    width = tile_side + 6
    span = tile_side * width
    result = jnp.zeros((chan_count, tile_count, span), jnp.float32)
    for row_shift in range(7):
        for col_shift in range(7):
            start = row_shift * width + col_shift
            result = result + weights[:, row_shift * 7 + col_shift][:, None, None] * flat[:, :, start:start + span].astype(jnp.float32)
    result = result.reshape(chan_count, tile_count, tile_side, width)[..., :tile_side]
    return result.reshape(chan_count, tile_count, tile_side * tile_side)

def kernel_grads(flat, gradient):
    chan_count = flat.shape[0]
    tile_count = flat.shape[1]
    tile_side = TS
    width = tile_side + 6
    span = tile_side * width
    wide = gradient.astype(jnp.float32).reshape(chan_count, tile_count, tile_side, tile_side)
    wide = jnp.pad(wide, ((0, 0), (0, 0), (0, 0), (0, 6))).reshape(chan_count, tile_count, span)
    columns = []
    for row_shift in range(7):
        for col_shift in range(7):
            start = row_shift * width + col_shift
            columns.append(lax.optimization_barrier(jnp.sum(wide * flat[:, :, start:start + span].astype(jnp.float32), axis=(1, 2))))
    return jnp.stack(columns, axis=1)

def gelu_value(hidden):
    return hidden * 0.5 * (1.0 + lax.erf(hidden * 0.7071067811865476))

def gelu_slope(hidden):
    return 0.5 * (1.0 + lax.erf(hidden * 0.7071067811865476)) + hidden * jnp.exp(-0.5 * hidden * hidden) * 0.3989422804014327

def pixel_block(columns, upstream_cols, gain, shift, weight_in, bias_in, weight_out, scale):
    values = columns.astype(jnp.float32)
    centered = values - lax.optimization_barrier(jnp.mean(values, axis=0, keepdims=True))
    inv_std = lax.rsqrt(lax.optimization_barrier(jnp.mean(centered * centered, axis=0, keepdims=True)) + 1e-06)
    normed = centered * inv_std
    inputs = (normed * gain[:, None] + shift[:, None]).astype(jnp.bfloat16)
    hidden = jnp.dot(weight_in, inputs, preferred_element_type=jnp.float32) + bias_in[:, None]
    activation = gelu_value(hidden).astype(jnp.bfloat16)
    mixed_out = jnp.dot(weight_out, activation, preferred_element_type=jnp.float32)
    branch = (scale[:, None] * mixed_out).astype(jnp.bfloat16)
    upstream = upstream_cols.astype(jnp.float32)
    grad_scale = lax.optimization_barrier(jnp.sum(upstream * mixed_out, axis=1))
    grad_mixed = (scale[:, None] * upstream).astype(jnp.bfloat16)
    grad_weight_out = lax.dot_general(grad_mixed, activation, (((1,), (1,)), ((), ())), preferred_element_type=jnp.float32)
    grad_act = lax.dot_general(weight_out, grad_mixed, (((0,), (0,)), ((), ())), preferred_element_type=jnp.float32)
    grad_hidden = grad_act * gelu_slope(hidden)
    grad_bias_in = lax.optimization_barrier(jnp.sum(grad_hidden, axis=1))
    hidden_grad = grad_hidden.astype(jnp.bfloat16)
    grad_weight_in = lax.dot_general(hidden_grad, inputs, (((1,), (1,)), ((), ())), preferred_element_type=jnp.float32)
    grad_inputs = lax.dot_general(weight_in, hidden_grad, (((0,), (0,)), ((), ())), preferred_element_type=jnp.float32)
    grad_gain = lax.optimization_barrier(jnp.sum(grad_inputs * normed, axis=1))
    grad_shift = lax.optimization_barrier(jnp.sum(grad_inputs, axis=1))
    grad_normed = grad_inputs * gain[:, None]
    grad_conv = (grad_normed - lax.optimization_barrier(jnp.mean(grad_normed, axis=0, keepdims=True)) - normed * lax.optimization_barrier(jnp.mean(grad_normed * normed, axis=0, keepdims=True))) * inv_std
    return (branch, grad_conv.astype(jnp.bfloat16), (grad_weight_in, grad_weight_out, grad_bias_in, grad_gain, grad_shift, grad_scale))

def reference(features, cotangent, neighbours, kernel, norm_gain, norm_shift, weight_in, bias_in, weight_out, layer_scale):
    pixels = TS * TS
    blank = jnp.zeros((C, 1, pixels), features.dtype)
    rim_table = pack_rims(jnp.concatenate([features, blank], axis=1))
    starts = jnp.arange(N_REGION, dtype=jnp.int32) * TILE_DEV

    def conv_block(start):
        center = lax.dynamic_slice_in_dim(features, start, TILE_DEV, 1)
        lookup = lax.dynamic_slice_in_dim(neighbours, start, TILE_DEV, 1)
        return depthwise(assemble(center, rim_table, lookup), kernel).astype(jnp.bfloat16)
    conv_out = lax.map(conv_block, starts)
    conv_cols = conv_out.transpose(1, 0, 2, 3).reshape(C, TILES * pixels)
    upstream_all = cotangent.reshape(C, TILES * pixels)
    block = TILE_DEV * pixels
    pixel_starts = jnp.arange(N_REGION, dtype=jnp.int32) * block

    def mlp_step(carry, start):
        columns = lax.dynamic_slice_in_dim(conv_cols, start, block, 1)
        upstream = lax.dynamic_slice_in_dim(upstream_all, start, block, 1)
        branch, grad_cols, parts = pixel_block(columns, upstream, norm_gain, norm_shift, weight_in, bias_in, weight_out, layer_scale)
        return (tuple((first + second for first, second in zip(carry, parts))), (branch, grad_cols))
    init = (jnp.zeros((HID, C), jnp.float32), jnp.zeros((C, HID), jnp.float32), jnp.zeros((HID,), jnp.float32), jnp.zeros((C,), jnp.float32), jnp.zeros((C,), jnp.float32), jnp.zeros((C,), jnp.float32))
    totals, (branches, gradients) = lax.scan(mlp_step, init, pixel_starts)
    branch_all = branches.transpose(1, 0, 2).reshape(C, TILES, pixels)
    output = (features.astype(jnp.float32) + branch_all.astype(jnp.float32)).astype(jnp.bfloat16)
    grad_all = gradients.transpose(1, 0, 2).reshape(C, TILES, pixels)
    grad_table = pack_rims(jnp.concatenate([grad_all, blank], axis=1))
    flipped = kernel[:, ::-1]

    def back_block(start):
        center = lax.dynamic_slice_in_dim(grad_all, start, TILE_DEV, 1)
        lookup = lax.dynamic_slice_in_dim(neighbours, start, TILE_DEV, 1)
        x_center = lax.dynamic_slice_in_dim(features, start, TILE_DEV, 1)
        upstream = lax.dynamic_slice_in_dim(cotangent, start, TILE_DEV, 1)
        input_part = (upstream.astype(jnp.float32) + depthwise(assemble(center, grad_table, lookup), flipped)).astype(jnp.bfloat16)
        kernel_part = kernel_grads(assemble(x_center, rim_table, lookup), center)
        return (input_part, kernel_part)
    input_parts, kernel_parts = lax.map(back_block, starts)
    input_grad = input_parts.transpose(1, 0, 2, 3).reshape(C, TILES, pixels)
    factor = 1.0 / math.sqrt(TILES * pixels)
    return (output, input_grad, totals[0] * factor, totals[1] * factor, totals[2] * factor, totals[3] * factor, totals[4] * factor, totals[5] * factor, lax.optimization_barrier(jnp.sum(kernel_parts, axis=0)) * factor)
```

```python
import math

import jax
import jax.numpy as jnp
from jax import lax
from jax.experimental import pallas as pl
from jax.experimental.pallas import tpu as pltpu
from jax.sharding import PartitionSpec as P

TS = 16
CH = 24
TILE = 16
PIX = 256
ROWS = CH * TILE
C = 384
HID = 1536
PART = 96
EXTRA = 16
F32 = jnp.float32
BF = jnp.bfloat16
NT = (((1,), (1,)), ((), ()))
NN = (((1,), (0,)), ((), ()))
VMEM_LIMIT = 48 * 1024 * 1024


def iota(shape, dim):
    return lax.broadcasted_iota(jnp.int32, shape, dim)


def dot(left, right, dims=NN):
    return lax.dot_general(left, right, dims, preferred_element_type=F32)


def eye(n):
    return (iota((n, n), 0) == iota((n, n), 1)).astype(F32).astype(BF)


def tile_major():
    column = iota((ROWS, ROWS), 1)
    target = (column & 15) * CH + (column >> 4)
    return (iota((ROWS, ROWS), 0) == target).astype(F32).astype(BF)


def chan_major():
    row = iota((ROWS, ROWS), 0)
    target = (row & 15) * CH + (row >> 4)
    return (iota((ROWS, ROWS), 1) == target).astype(F32).astype(BF)


def fill_padded(pad, own, low, high, lookup):
    identity = eye(PIX)
    own_t = dot(identity, own, NT)
    own_b = own_t.astype(BF)
    low_b = dot(identity, low, NT).astype(BF)
    high_b = dot(identity, high, NT).astype(BF)
    row = iota((ROWS, 128), 0)
    lane = iota((ROWS, 128), 1)
    key = jnp.where(((row >> 4) & 7) == (lane >> 4), (row >> 7) * 16 + (row & 15), -1)

    def pick(directions):
        parts = [
            (key == lookup[d : d + 1, :]).astype(F32).astype(BF) for d in directions
        ]
        return jnp.concatenate(parts, axis=1)

    north = pick((0, 4, 5))
    south = pick((1, 6, 7))
    sides = pick((2, 3))
    for g in range(3):
        lanes = slice(g * 128, (g + 1) * 128)
        table = jnp.concatenate([low_b[:, lanes], own_b[:, lanes], high_b[:, lanes]], axis=1)
        top = dot(table[208:256], north)
        bottom = dot(table[0:48], south)
        side = dot(table, sides)
        pad[g, 3:19, 3:19, :] = own_t[:, lanes].reshape(16, 16, 128)
        pad[g, 0:3, 3:19, :] = top[:, 0:128].reshape(3, 16, 128)
        pad[g, 0:3, 0:3, :] = top[:, 128:256].reshape(3, 16, 128)[:, 13:16]
        pad[g, 0:3, 19:22, :] = top[:, 256:384].reshape(3, 16, 128)[:, 0:3]
        pad[g, 19:22, 3:19, :] = bottom[:, 0:128].reshape(3, 16, 128)
        pad[g, 19:22, 0:3, :] = bottom[:, 128:256].reshape(3, 16, 128)[:, 13:16]
        pad[g, 19:22, 19:22, :] = bottom[:, 256:384].reshape(3, 16, 128)[:, 0:3]
        pad[g, 3:19, 0:3, :] = side[:, 0:128].reshape(16, 16, 128)[:, 13:16]
        pad[g, 3:19, 19:22, :] = side[:, 128:256].reshape(16, 16, 128)[:, 0:3]


def convolve(pad, weights, result, flip):
    def group(g, carry):
        for half in range(2):
            total = [None] * TS
            for b in range(7):
                taps = [
                    weights[g, pl.ds((48 - 7 * a - b) if flip else (7 * a + b), 1), :]
                    for a in range(7)
                ]
                taps = [jnp.broadcast_to(t, (8, 128)) for t in taps]
                for r in range(22):
                    value = pad[g, r, pl.ds(b + 8 * half, 8), :]
                    for a in range(7):
                        i = r - a
                        if 0 <= i < TS:
                            term = taps[a] * value
                            total[i] = term if total[i] is None else total[i] + term
            for i in range(TS):
                result[g, i, pl.ds(8 * half, 8), :] = total[i]
        return carry

    lax.fori_loop(0, 3, group, 0)


def rows_of(result):
    return jnp.concatenate([result[g].reshape(PIX, 128) for g in range(3)], axis=1)


def forward_kernel(own, low, high, lookup, weights, conv, pad, result):
    fill_padded(pad, own[...], low[...], high[...], lookup)
    convolve(pad, weights, result, False)
    conv[...] = dot(tile_major(), rows_of(result).astype(BF), NT).astype(BF)


def backward_kernel(
    received, low, high, lookup, weights, features, cotangent, pad_x,
    output, input_grad, kernel_grad, pad, result, gradient, sums,
):
    order = chan_major()
    both = dot(order, received[...])
    output[...] = (features[...].astype(F32) + both[:, :PIX]).astype(BF)
    own = both[:, PIX:].astype(BF)
    low_rows = dot(order, low[...]).astype(BF)
    high_rows = dot(order, high[...]).astype(BF)
    fill_padded(pad, own, low_rows, high_rows, lookup)
    convolve(pad, weights, result, True)
    upstream = dot(eye(PIX), cotangent[...], NT)
    total = (upstream + rows_of(result)).astype(BF)
    input_grad[...] = dot(eye(ROWS), total, NT).astype(BF)
    for g in range(3):
        gradient[g] = pad[g, 3:19, 3:19, :]
    sums[...] = jnp.zeros_like(sums)

    def group(g, carry):
        for b in range(7):
            total = [None] * 7
            for half in range(2):
                grads = [gradient[g, i, pl.ds(8 * half, 8), :] for i in range(TS)]
                for r in range(22):
                    value = pad_x[g, r, pl.ds(b + 8 * half, 8), :]
                    for a in range(7):
                        i = r - a
                        if 0 <= i < TS:
                            term = grads[i] * value
                            total[a] = term if total[a] is None else total[a] + term
            for a in range(7):
                sums[g, pl.ds(7 * a + b, 1), :] = jnp.sum(total[a], axis=0, keepdims=True)
        return carry

    lax.fori_loop(0, 3, group, 0)
    spread = jnp.concatenate([sums[g] for g in range(3)], axis=1)
    member = (iota((32, ROWS), 0) == (iota((32, ROWS), 1) >> 4)).astype(F32)
    kernel_grad[...] = lax.dot_general(
        member, spread, NT, preferred_element_type=F32, precision=lax.Precision.HIGHEST
    )


def pixel_kernel(
    core, columns, upstream_cols, gain, shift, scale, bias,
    weight_in, weight_in_t, weight_out, weight_out_t,
    out, keep, send, mixed_ref,
):
    own = core[0]
    values = columns[...].astype(F32)
    centered = values - jnp.mean(values, axis=0, keepdims=True)
    inv_std = lax.rsqrt(jnp.mean(centered * centered, axis=0, keepdims=True) + 1e-06)
    normed = centered * inv_std
    inputs = (normed * gain[...] + shift[...]).astype(BF)
    upstream = upstream_cols[...].astype(F32)
    mixed_ref[...] = (scale[...] * upstream).astype(BF)
    grad_mixed = mixed_ref[...]
    lane = iota((C, 128), 1)
    small = jnp.zeros((C, 128), F32)
    mixed_out = jnp.zeros((C, PIX), F32)
    grad_inputs = jnp.zeros((C, PIX), F32)
    for k in range(4):
        block = (2 * own + k) if k < 2 else (2 * (1 - own) + k - 2)
        rows = pl.ds(pl.multiple_of(block * C, C), C)
        hidden = dot(weight_in[rows, :], inputs) + bias[rows, :]
        cdf = 0.5 + 0.5 * lax.erf(hidden * 0.7071067811865476)
        activation = (hidden * cdf).astype(BF)
        slope = cdf + hidden * jnp.exp(-0.5 * hidden * hidden) * 0.3989422804014327
        mixed_out = mixed_out + dot(weight_out[:, rows], activation)
        grad_hidden = dot(weight_out_t[rows, :], grad_mixed) * slope
        small = small + jnp.where(
            lane == block, jnp.sum(grad_hidden, axis=1, keepdims=True), 0.0
        )
        hidden_grad = grad_hidden.astype(BF)
        grad_inputs = grad_inputs + dot(weight_in_t[:, rows], hidden_grad)
        part = dot(hidden_grad, inputs, NT).astype(BF)
        target = keep if k < 2 else send
        for s in range(4):
            target[(k % 2) * 4 + s, 0:PART, :] = part[s * PART : (s + 1) * PART]
        for ref, side in ((keep, own), (send, 1 - own)):
            some = mixed_ref[pl.ds(pl.multiple_of(side * 192, 192), 192), :]
            part = dot(some, activation, NT).astype(BF)
            for s in range(2):
                ref[8 + 2 * block + s, 0:PART, :] = part[s * PART : (s + 1) * PART]
    branch = (scale[...] * mixed_out).astype(BF)
    grad_scale = jnp.sum(upstream * mixed_out, axis=1, keepdims=True)
    grad_gain = jnp.sum(grad_inputs * normed, axis=1, keepdims=True)
    grad_shift = jnp.sum(grad_inputs, axis=1, keepdims=True)
    grad_normed = grad_inputs * gain[...]
    grad_conv = (
        grad_normed
        - jnp.mean(grad_normed, axis=0, keepdims=True)
        - normed * jnp.mean(grad_normed * normed, axis=0, keepdims=True)
    ) * inv_std
    out[:, :PIX] = branch
    out[:, PIX:] = grad_conv.astype(BF)
    small = small + jnp.where(lane == 4, grad_gain, 0.0)
    small = small + jnp.where(lane == 5, grad_shift, 0.0)
    small = small + jnp.where(lane == 6, grad_scale, 0.0)
    small_rows = jnp.transpose(small)[0:8]
    high = small_rows.astype(BF).astype(F32)
    extra = jnp.concatenate([high, small_rows - high], axis=0).astype(BF)
    for ref in (keep, send):
        ref[0, PART:, :] = extra
        for j in range(1, 16):
            ref[j, PART:, :] = jnp.zeros((EXTRA, C), BF)


def finish_kernel(factor, core, mine, other, grad_in, grad_out):
    own = core[0]
    for ref, side in ((mine, own), (other, 1 - own)):
        for j in range(8):
            rows = pl.ds(pl.multiple_of(side * 768 + j * PART, PART), PART)
            grad_in[rows, :] = ref[j, 0:PART, :].astype(F32) * factor
        for q in range(4):
            for s in range(2):
                rows = pl.ds(pl.multiple_of(side * 192 + s * PART, PART), PART)
                grad_out[rows, q * C : (q + 1) * C] = (
                    ref[8 + 2 * q + s, 0:PART, :].astype(F32) * factor
                )


def call(body, shapes, scratch, args, name, flops, scalar_first=False):
    vmem = pl.BlockSpec(memory_space=pltpu.VMEM)
    smem = pl.BlockSpec(memory_space=pltpu.SMEM)
    specs = [smem if scalar_first and i == 0 else vmem for i in range(len(args))]
    moved = sum(a.size * a.dtype.itemsize for a in args)
    moved += sum(math.prod(s) * jnp.dtype(d).itemsize for s, d in shapes)
    return pl.pallas_call(
        body,
        out_shape=[jax.ShapeDtypeStruct(s, d) for s, d in shapes],
        in_specs=specs,
        out_specs=[vmem] * len(shapes),
        scratch_shapes=[pltpu.VMEM(s, d) for s, d in scratch],
        compiler_params=pltpu.CompilerParams(vmem_limit_bytes=VMEM_LIMIT),
        cost_estimate=pl.CostEstimate(flops=flops, bytes_accessed=moved, transcendentals=0),
        name=name,
    )(*args)


def shifted(field):
    count = lax.axis_size("region")
    forward = [(i, i + 1) for i in range(count - 1)]
    backward = [(i + 1, i) for i in range(count - 1)]
    return lax.ppermute(field, "region", forward), lax.ppermute(field, "region", backward)


def cube_pairs(count, bit):
    ring = count // 2
    label = [z ^ (z >> 1) for z in range(ring)]
    place = {g: z for z, g in enumerate(label)}
    return [(2 * z + c, 2 * place[label[z] ^ bit] + c) for z in range(ring) for c in range(2)]


def per_device(
    features, cotangent, neighbours, kernel, norm_gain, norm_shift,
    weight_in, bias_in, weight_out, layer_scale,
):
    count = lax.axis_size("region")
    peers = lax.axis_size("chan")
    region = lax.axis_index("region")
    core = (region & 1).astype(jnp.int32).reshape(1)
    total_tiles = TILE * count
    factor = 1.0 / math.sqrt(total_tiles * PIX)
    swap = [(i, i ^ 1) for i in range(count)]

    x = features.reshape(ROWS, PIX)
    upstream = cotangent.reshape(ROWS, PIX)
    x_low, x_high = shifted(x)
    first_tile = (region - 1) * TILE
    lookup = jnp.where(neighbours >= total_tiles, 3 * TILE, neighbours - first_tile)
    lookup = jnp.tile(lookup, (1, 8))
    weights = jnp.repeat(kernel.reshape(3, 8, 49).transpose(0, 2, 1), TILE, axis=2)
    upstream_cols = lax.all_to_all(
        cotangent, "chan", split_axis=1, concat_axis=0, tiled=True
    ).reshape(C, PIX)

    conv, pad_x = call(
        forward_kernel,
        [((ROWS, PIX), BF), ((3, 22, 24, 128), F32)],
        [((3, 16, 16, 128), F32)],
        (x, x_low, x_high, lookup, weights),
        "forward_conv",
        400_000_000,
    )
    columns = lax.all_to_all(conv, "chan", split_axis=0, concat_axis=0, tiled=True)

    out, keep, send = call(
        pixel_kernel,
        [((C, 2 * PIX), BF), ((16, PART + EXTRA, C), BF), ((16, PART + EXTRA, C), BF)],
        [((C, PIX), BF)],
        (
            core, columns, upstream_cols,
            norm_gain.reshape(C, 1), norm_shift.reshape(C, 1), layer_scale.reshape(C, 1),
            bias_in.reshape(HID, 1),
            weight_in, weight_in.T, weight_out, weight_out.T,
        ),
        "pixel_block",
        2_000_000_000,
        True,
    )
    partner = lax.ppermute(send, "region", swap)
    received = lax.all_to_all(out, "chan", split_axis=0, concat_axis=0, tiled=True)
    half = (keep.astype(F32) + partner.astype(F32)).astype(BF)
    half = lax.all_to_all(half, "chan", split_axis=0, concat_axis=0, tiled=True)
    half = jnp.sum(half.astype(F32), axis=0)

    grad_low, grad_high = shifted(received[:, PIX:])
    output, input_grad, kernel_part = call(
        backward_kernel,
        [((ROWS, PIX), BF), ((ROWS, PIX), BF), ((32, 64), F32)],
        [
            ((3, 22, 24, 128), F32),
            ((3, 16, 16, 128), F32),
            ((3, 16, 16, 128), F32),
            ((3, 64, 128), F32),
        ],
        (received, grad_low, grad_high, lookup, weights, x, upstream, pad_x),
        "backward_conv",
        800_000_000,
    )

    def split(value):
        high = value.astype(BF)
        return high, (value - high.astype(F32)).astype(BF)

    high, low = split(kernel_part)
    pair = jnp.concatenate([high, low], axis=1)
    other = lax.ppermute(pair, "region", swap)
    joined = pair.astype(F32) + other.astype(F32)
    kernel_part = joined[:, :64] + joined[:, 64:]

    for bit in (1, 2, 4):
        high, low = split(kernel_part)
        tail = jnp.concatenate([high, low, jnp.zeros((32, C - 128), BF)], axis=1)
        sent = jnp.concatenate([half.astype(BF), tail], axis=0)
        got = lax.ppermute(sent, "region", cube_pairs(count, bit))
        joined = sent.astype(F32) + got.astype(F32)
        half = joined[: PART + EXTRA]
        kernel_part = joined[PART + EXTRA :, :64] + joined[PART + EXTRA :, 64:128]

    mine = jnp.broadcast_to(half.astype(BF)[None], (peers, PART + EXTRA, C))
    mine = lax.all_to_all(mine, "chan", split_axis=0, concat_axis=0, tiled=True)
    other = lax.ppermute(mine, "region", swap)
    grad_weight_in, grad_weight_out = call(
        lambda *refs: finish_kernel(factor, *refs),
        [((HID, C), F32), ((C, HID), F32)],
        [],
        (core, mine, other),
        "finish",
        2_000_000,
        True,
    )
    small = (mine[0, PART : PART + 8].astype(F32) + mine[0, PART + 8 :].astype(F32)) * factor
    return (
        output.reshape(features.shape),
        input_grad.reshape(features.shape),
        grad_weight_in,
        grad_weight_out,
        small[0:4].reshape(HID),
        small[4],
        small[5],
        small[6],
        kernel_part[:CH, :49] * factor,
    )


def solution(mesh):
    block = P("chan", "region", None)
    in_specs = (block, block, P(None, "region"), P("chan", None)) + (P(),) * 6
    out_specs = (block, block) + (P(),) * 6 + (P("chan", None),)
    return jax.shard_map(
        per_device, mesh=mesh, in_specs=in_specs, out_specs=out_specs, check_vma=False
    )
```

```python
import functools
import math

import jax
import jax.numpy as jnp
from jax import lax
from jax.experimental import pallas as pl
from jax.experimental.pallas import tpu as pltpu
from jax.sharding import PartitionSpec as P

TS = 16
CH = 24
TILE = 16
PIX = 256
ROWS = CH * TILE
C = 384
HID = 1536
PART = 96
EXTRA = 8
LONG = PART + EXTRA
BRANCH = 32
F32 = jnp.float32
BF = jnp.bfloat16
NT = (((1,), (1,)), ((), ()))
NN = (((1,), (0,)), ((), ()))


def iota(shape, dim):
    return lax.broadcasted_iota(jnp.int32, shape, dim)


def dot(left, right, dims=NN):
    return lax.dot_general(left, right, dims, preferred_element_type=F32)


def eye(n):
    return (iota((n, n), 0) == iota((n, n), 1)).astype(F32).astype(BF)


def tile_major():
    column = iota((ROWS, ROWS), 1)
    target = (column & 15) * CH + (column >> 4)
    return (iota((ROWS, ROWS), 0) == target).astype(F32).astype(BF)


def chan_major():
    row = iota((ROWS, ROWS), 0)
    target = (row & 15) * CH + (row >> 4)
    return (iota((ROWS, ROWS), 1) == target).astype(F32).astype(BF)


def fill_padded(pad, own, low, high, lookup):
    identity = eye(PIX)
    own_t = dot(identity, own, NT)
    own_b = own_t.astype(BF)
    low_b = dot(identity, low, NT).astype(BF)
    high_b = dot(identity, high, NT).astype(BF)
    row = iota((ROWS, 128), 0)
    lane = iota((ROWS, 128), 1)
    key = jnp.where(((row >> 4) & 7) == (lane >> 4), (row >> 7) * 16 + (row & 15), -1)

    def pick(directions):
        parts = [
            (key == lookup[d : d + 1, :]).astype(F32).astype(BF) for d in directions
        ]
        return jnp.concatenate(parts, axis=1)

    north = pick((0, 4, 5))
    south = pick((1, 6, 7))
    sides = pick((2, 3))
    for g in range(3):
        lanes = slice(g * 128, (g + 1) * 128)
        table = jnp.concatenate([low_b[:, lanes], own_b[:, lanes], high_b[:, lanes]], axis=1)
        top = dot(table[208:256], north)
        bottom = dot(table[0:48], south)
        side = dot(table, sides)
        pad[g, 3:19, 3:19, :] = own_t[:, lanes].reshape(16, 16, 128)
        pad[g, 0:3, 3:19, :] = top[:, 0:128].reshape(3, 16, 128)
        pad[g, 0:3, 0:3, :] = top[:, 128:256].reshape(3, 16, 128)[:, 13:16]
        pad[g, 0:3, 19:22, :] = top[:, 256:384].reshape(3, 16, 128)[:, 0:3]
        pad[g, 19:22, 3:19, :] = bottom[:, 0:128].reshape(3, 16, 128)
        pad[g, 19:22, 0:3, :] = bottom[:, 128:256].reshape(3, 16, 128)[:, 13:16]
        pad[g, 19:22, 19:22, :] = bottom[:, 256:384].reshape(3, 16, 128)[:, 0:3]
        pad[g, 3:19, 0:3, :] = side[:, 0:128].reshape(16, 16, 128)[:, 13:16]
        pad[g, 3:19, 19:22, :] = side[:, 128:256].reshape(16, 16, 128)[:, 0:3]


def lookup_rows(region, neighbours, total):
    raw = neighbours[...]
    place = jnp.where(raw >= total, 3 * TILE, raw - (region[0] - 1) * TILE)
    repeat = ((iota((TILE, 128), 1) & 15) == iota((TILE, 128), 0)).astype(F32)
    return dot(place.astype(F32), repeat).astype(jnp.int32)


def spread_taps(kernel, weights):
    member = (iota((CH, ROWS), 0) == (iota((CH, ROWS), 1) >> 4)).astype(F32)
    wide = lax.dot_general(
        kernel[...], member, (((0,), (0,)), ((), ())),
        preferred_element_type=F32, precision=lax.Precision.HIGHEST,
    )
    for g in range(3):
        weights[g] = wide[:, g * 128 : (g + 1) * 128]


def convolve(pad, weights, result, flip):
    def group(g, carry):
        for half in range(2):
            total = [None] * TS
            for b in range(7):
                taps = [
                    weights[g, pl.ds((48 - 7 * a - b) if flip else (7 * a + b), 1), :]
                    for a in range(7)
                ]
                taps = [jnp.broadcast_to(t, (8, 128)) for t in taps]
                for r in range(22):
                    value = pad[g, r, pl.ds(b + 8 * half, 8), :]
                    for a in range(7):
                        i = r - a
                        if 0 <= i < TS:
                            term = taps[a] * value
                            total[i] = term if total[i] is None else total[i] + term
            for i in range(TS):
                result[g, i, pl.ds(8 * half, 8), :] = total[i]
        return carry

    lax.fori_loop(0, 3, group, 0)


def rows_of(result):
    return jnp.concatenate([result[g].reshape(PIX, 128) for g in range(3)], axis=1)


def forward_kernel(
    total, region, own, low, high, neighbours, kernel, cotangent, both, pad_out,
    pad, result, weights, own_ref, low_ref, high_ref, neighbours_ref, kernel_ref,
    cotangent_ref, sems,
):
    pairs = [
        (kernel, kernel_ref), (neighbours, neighbours_ref), (own, own_ref),
        (low, low_ref), (high, high_ref), (cotangent, cotangent_ref),
    ]
    loads = [pltpu.make_async_copy(*pair, sems.at[i]) for i, pair in enumerate(pairs)]
    for load in loads:
        load.start()
    order = tile_major()
    loads[0].wait()
    spread_taps(kernel_ref, weights)
    for load in loads[1:5]:
        load.wait()
    lookup = lookup_rows(region, neighbours_ref, total)
    fill_padded(pad, own_ref[...], low_ref[...], high_ref[...], lookup)
    store = pltpu.make_async_copy(pad, pad_out, sems.at[6])
    store.start()
    convolve(pad, weights, result, False)
    both[:, :PIX] = dot(order, rows_of(result).astype(BF), NT).astype(BF)
    loads[5].wait()
    both[:, PIX:] = dot(order, cotangent_ref[...]).astype(BF)
    store.wait()


def taps_kernel(
    received, features, pad_x, output, grad, kernel_grad, unpacked, gradient, sums
):
    for t in range(TILE):
        part = received[t, 0:BRANCH, :].astype(F32)
        rows = slice(t * CH, (t + 1) * CH)
        unpacked[rows, 0:384] = part[0:CH]
        for i in range(3):
            piece = part[CH:, i * 128 : (i + 1) * 128]
            unpacked[t * CH + 8 * i : t * CH + 8 * (i + 1), 384:512] = piece
    both = dot(chan_major(), unpacked[...].astype(BF))
    output[...] = (features[...].astype(F32) + both[:, :PIX]).astype(BF)
    own_grad = both[:, PIX:].astype(BF)
    grad[...] = own_grad
    own = dot(eye(PIX), own_grad, NT)
    for g in range(3):
        gradient[g] = own[:, g * 128 : (g + 1) * 128].reshape(TS, TS, 128)
    sums[...] = jnp.zeros_like(sums)

    def group(g, carry):
        for b in range(7):
            total = [None] * 7
            for half in range(2):
                grads = [gradient[g, i, pl.ds(8 * half, 8), :] for i in range(TS)]
                for r in range(22):
                    value = pad_x[g, r, pl.ds(b + 8 * half, 8), :]
                    for a in range(7):
                        i = r - a
                        if 0 <= i < TS:
                            term = grads[i] * value
                            total[a] = term if total[a] is None else total[a] + term
            for a in range(7):
                sums[g, pl.ds(7 * a + b, 1), :] = jnp.sum(total[a], axis=0, keepdims=True)
        return carry

    lax.fori_loop(0, 3, group, 0)
    spread = jnp.concatenate([sums[g] for g in range(3)], axis=1)
    member = (iota((32, ROWS), 0) == (iota((32, ROWS), 1) >> 4)).astype(F32)
    total = lax.dot_general(
        member, spread, NT, preferred_element_type=F32, precision=lax.Precision.HIGHEST
    )
    kernel_grad[...] = halves_of(jnp.concatenate([total[8 * i : 8 * i + 8] for i in range(3)], axis=1))


def halves_of(value):
    high = value.astype(BF).astype(F32)
    return jnp.concatenate([high, value - high], axis=1).astype(BF)


def backward_kernel(
    total_tiles, region, own, low, high, neighbours, kernel, cotangent, input_grad,
    pad, result, weights,
):
    spread_taps(kernel, weights)
    lookup = lookup_rows(region, neighbours, total_tiles)
    fill_padded(pad, own[...], low[...], high[...], lookup)
    convolve(pad, weights, result, True)
    upstream = dot(eye(PIX), cotangent[...], NT)
    total = (upstream + rows_of(result)).astype(BF)
    input_grad[...] = dot(eye(ROWS), total, NT).astype(BF)


def normalize(columns):
    values = columns[:, :PIX].astype(F32)
    centered = values - jnp.mean(values, axis=0, keepdims=True)
    inv_std = lax.rsqrt(jnp.mean(centered * centered, axis=0, keepdims=True) + 1e-06)
    return centered * inv_std, inv_std


def hidden_blocks(
    side, table, inputs, grad_mixed, bias, weight_in, weight_in_t, weight_out, weight_out_t,
    parts, mixed_out, grad_inputs, small,
):
    lane = iota((C, 128), 1)
    for q in range(4):
        bias[q * C : (q + 1) * C, :] = table[:, q : q + 1]
    for k in range(2):
        block = 2 * side + k
        rows = pl.ds(pl.multiple_of(block * C, C), C)
        hidden = dot(weight_in[rows, :], inputs) + bias[rows, :]
        cdf = 0.5 + 0.5 * lax.erf(hidden * 0.7071067811865476)
        activation = (hidden * cdf).astype(BF)
        slope = cdf + hidden * jnp.exp(-0.5 * hidden * hidden) * 0.3989422804014327
        mixed_out = mixed_out + dot(weight_out[:, rows], activation)
        grad_hidden = dot(weight_out_t[rows, :], grad_mixed) * slope
        small = small + jnp.where(
            lane == block, jnp.sum(grad_hidden, axis=1, keepdims=True), 0.0
        )
        hidden_grad = grad_hidden.astype(BF)
        grad_inputs = grad_inputs + dot(weight_in_t[:, rows], hidden_grad)
        part = dot(hidden_grad, inputs, NT).astype(BF)
        for s in range(4):
            parts[4 * k + s] = part[s * PART : (s + 1) * PART]
        part = dot(grad_mixed, activation, NT).astype(BF)
        for s in range(4):
            parts[8 + 4 * k + s] = part[s * PART : (s + 1) * PART]
    return mixed_out, grad_inputs, small


def first_half_kernel(
    region, columns, vectors, weight_in, weight_in_t, weight_out, weight_out_t,
    parts, mixed_sum, grad_sum, small_sum, bias, late, sem,
):
    load = pltpu.make_async_copy(weight_out_t, late, sem)
    load.start()
    table = jnp.transpose(vectors[...])
    normed, _ = normalize(columns)
    inputs = (normed * table[:, 4:5] + table[:, 5:6]).astype(BF)
    grad_mixed = (table[:, 6:7] * columns[:, PIX:].astype(F32)).astype(BF)
    zeros = jnp.zeros((C, PIX), F32)
    load.wait()
    mixed_sum[...], grad_sum[...], small_sum[...] = hidden_blocks(
        1 - (region[0] & 1), table, inputs, grad_mixed, bias,
        weight_in, weight_in_t, weight_out, late,
        parts, zeros, zeros, jnp.zeros((C, 128), F32),
    )


def second_half_kernel(
    region, columns, vectors, weight_in, weight_in_t, weight_out, weight_out_t,
    mixed_sum, grad_sum, small_sum, out, parts, extra, bias, late, sem,
):
    load = pltpu.make_async_copy(weight_out_t, late, sem)
    load.start()
    table = jnp.transpose(vectors[...])
    gain = table[:, 4:5]
    scale = table[:, 6:7]
    normed, inv_std = normalize(columns)
    inputs = (normed * gain + table[:, 5:6]).astype(BF)
    upstream = columns[:, PIX:].astype(F32)
    grad_mixed = (scale * upstream).astype(BF)
    load.wait()
    mixed_out, grad_inputs, small = hidden_blocks(
        region[0] & 1, table, inputs, grad_mixed, bias,
        weight_in, weight_in_t, weight_out, late,
        parts, mixed_sum[...], grad_sum[...], small_sum[...],
    )
    branch = scale * mixed_out
    grad_scale = jnp.sum(upstream * mixed_out, axis=1, keepdims=True)
    grad_gain = jnp.sum(grad_inputs * normed, axis=1, keepdims=True)
    grad_shift = jnp.sum(grad_inputs, axis=1, keepdims=True)
    grad_normed = grad_inputs * gain
    grad_conv = (
        grad_normed
        - jnp.mean(grad_normed, axis=0, keepdims=True)
        - normed * jnp.mean(grad_normed * normed, axis=0, keepdims=True)
    ) * inv_std
    for j in range(16):
        rows = slice(j * CH, (j + 1) * CH)
        side = grad_conv[rows, 128:]
        first = jnp.concatenate([branch[rows], grad_conv[rows, :128]], axis=1)
        last = jnp.concatenate([side[8 * i : 8 * i + 8] for i in range(3)], axis=1)
        out[j] = jnp.concatenate([first, last], axis=0).astype(BF)
    lane = iota((C, 128), 1)
    small = small + jnp.where(lane == 4, grad_gain, 0.0)
    small = small + jnp.where(lane == 5, grad_shift, 0.0)
    small = small + jnp.where(lane == 6, grad_scale, 0.0)
    extra[...] = jnp.transpose(small)[0:EXTRA].astype(BF)


def add_kernel(out, first, second, extra, total):
    total[:, 0:BRANCH, :] = out[...]
    total[:, BRANCH : BRANCH + PART, :] = (
        first[...].astype(F32) + second[...].astype(F32)
    ).astype(BF)
    total[0, BRANCH + PART :, :] = extra[...]
    total[1:, BRANCH + PART :, :] = jnp.zeros((15, EXTRA, C), BF)


def first_step_kernel(sent, got, kernel_grad, total):
    total[0:LONG, :] = (sent[...].astype(F32) + got[...].astype(F32)).astype(BF)
    total[LONG:, :] = kernel_grad[...]


def joined(sent, got):
    value = sent[...].astype(F32) + got[...].astype(F32)
    return value[0:LONG].astype(BF), value[LONG:, :192] + value[LONG:, 192:]


def next_step_kernel(sent, got, total):
    weights, taps = joined(sent, got)
    total[0:LONG, :] = weights
    total[LONG:, :] = halves_of(taps)


def spread_kernel(sent, got, total, kernel_grad):
    weights, taps = joined(sent, got)
    kernel_grad[...] = taps
    for j in range(16):
        total[j] = weights


def place(factor, side, ref, grad_in, grad_out, tall, wide, sems):
    half = pl.multiple_of(side * 768, 768)
    for j in range(8):
        tall[j * PART : (j + 1) * PART, :] = ref[j, 0:PART, :].astype(F32) * factor
    first = pltpu.make_async_copy(tall, grad_in.at[pl.ds(half, 768), :], sems.at[0])
    first.start()
    for k in range(2):
        for s in range(4):
            wide[s * PART : (s + 1) * PART, k * C : (k + 1) * C] = (
                ref[8 + 4 * k + s, 0:PART, :].astype(F32) * factor
            )
    second = pltpu.make_async_copy(wide, grad_out.at[:, pl.ds(half, 768)], sems.at[1])
    second.start()
    first.wait()
    second.wait()


def place_own_kernel(factor, region, ref, grad_in, grad_out, tall, wide, sems):
    place(factor, region[0] & 1, ref, grad_in, grad_out, tall, wide, sems)


def place_other_kernel(factor, region, ref, in_a, out_a, grad_in, grad_out, tall, wide, sems):
    place(factor, 1 - (region[0] & 1), ref, grad_in, grad_out, tall, wide, sems)


def call(body, shapes, scratch, args, name, flops, limit, smem=(), far=(), aliases=None):
    spaces = [
        pl.BlockSpec(memory_space=pltpu.SMEM if i in smem else pltpu.HBM if i in far else pltpu.VMEM)
        for i in range(len(args) + len(shapes))
    ]
    moved = sum(a.size * a.dtype.itemsize for a in args)
    moved += sum(math.prod(s) * jnp.dtype(d).itemsize for s, d in shapes)
    return pl.pallas_call(
        body,
        out_shape=[jax.ShapeDtypeStruct(s, d) for s, d in shapes],
        in_specs=spaces[: len(args)],
        out_specs=spaces[len(args) :],
        scratch_shapes=[
            pltpu.SemaphoreType.DMA(s) if d is None else pltpu.VMEM(s, d) for s, d in scratch
        ],
        compiler_params=pltpu.CompilerParams(vmem_limit_bytes=limit * 1024 * 1024),
        cost_estimate=pl.CostEstimate(flops=flops, bytes_accessed=moved, transcendentals=0),
        input_output_aliases=aliases or {},
        name=name,
    )(*args)


def shifted(field):
    count = lax.axis_size("region")
    forward = [(i, i + 1) for i in range(count - 1)]
    backward = [(i + 1, i) for i in range(count - 1)]
    return lax.ppermute(field, "region", forward), lax.ppermute(field, "region", backward)


def cube_pairs(count, bit, core=0):
    ring = count // 2
    label = [z ^ (z >> 1) for z in range(ring)]
    place = {g: z for z, g in enumerate(label)}
    return [
        (2 * z + c, 2 * place[label[z] ^ bit] + (c ^ core)) for z in range(ring) for c in range(2)
    ]


def sum_four(value, first, second, both):
    near, far, across = (lax.ppermute(value, "region", pairs) for pairs in (first, second, both))
    return (value + near) + (far + across)


def per_device(
    features, cotangent, neighbours, kernel, norm_gain, norm_shift,
    weight_in, bias_in, weight_out, layer_scale,
):
    count = lax.axis_size("region")
    peers = lax.axis_size("chan")
    region = lax.axis_index("region").astype(jnp.int32).reshape(1)
    total_tiles = TILE * count
    factor = 1.0 / math.sqrt(total_tiles * PIX)
    swap = [(i, i ^ 1) for i in range(count)]

    x = features.reshape(ROWS, PIX)
    upstream = cotangent.reshape(ROWS, PIX)
    x_low, x_high = shifted(x)
    vectors = jnp.concatenate(
        [
            bias_in.reshape(4, C), norm_gain[None], norm_shift[None], layer_scale[None],
            jnp.zeros((1, C), F32),
        ],
        axis=0,
    )

    padded = ((3, 22, 24, 128), F32)
    square = ((3, 16, 16, 128), F32)
    taps = ((3, 49, 128), F32)
    block = ((ROWS, PIX), BF)
    columns, pad_x = call(
        functools.partial(forward_kernel, total_tiles),
        [((ROWS, 2 * PIX), BF), padded],
        [
            padded, square, taps, block, block, block, ((8, TILE), jnp.int32), ((CH, 49), F32),
            block, ((7,), None),
        ],
        (region, x, x_low, x_high, neighbours, kernel, upstream),
        "forward_conv",
        400_000_000,
        56,
        smem=(0,),
        far=(1, 2, 3, 4, 5, 6, 8),
    )
    columns = lax.all_to_all(columns, "chan", split_axis=0, concat_axis=0, tiled=True)

    halves = (16, PART, C)
    pixels = (region, columns, vectors, weight_in, weight_in.T, weight_out, weight_out.T)
    scratch = [((HID, 1), F32), ((HID, C), BF), ((), None)]
    sums = [((C, PIX), F32), ((C, PIX), F32), ((C, 128), F32)]
    send, *partial = call(
        first_half_kernel,
        [(halves, BF)] + sums,
        scratch,
        pixels,
        "pixels_first",
        1_000_000_000,
        24,
        smem=(0,),
        far=(6,),
    )
    partner = lax.ppermute(send, "region", swap)
    out, keep, extra = call(
        second_half_kernel,
        [((16, BRANCH, C), BF), (halves, BF), ((EXTRA, C), BF)],
        scratch,
        (*pixels, *partial),
        "pixels_second",
        1_000_000_000,
        24,
        smem=(0,),
        far=(6,),
    )
    (travel,) = call(
        add_kernel, [((16, BRANCH + LONG, C), BF)], [], (out, keep, partner, extra),
        "add_cores", 1_000_000, 8,
    )
    travel = lax.all_to_all(travel, "chan", split_axis=0, concat_axis=0, tiled=True)

    sent = jnp.sum(travel[:, BRANCH:].astype(F32), axis=0).astype(BF)
    got = lax.ppermute(sent, "region", cube_pairs(count, 1))
    output, grad, kernel_part = call(
        taps_kernel,
        [((ROWS, PIX), BF), ((ROWS, PIX), BF), ((8, C), BF)],
        [((ROWS, 2 * PIX), F32), square, ((3, 64, 128), F32)],
        (travel, x, pad_x),
        "kernel_taps",
        400_000_000,
        16,
    )
    step = [((LONG + 8, C), BF)]
    (sent,) = call(first_step_kernel, step, [], (sent, got, kernel_part), "step", 100_000, 4)
    got = lax.ppermute(sent, "region", cube_pairs(count, 2))
    (sent,) = call(next_step_kernel, step, [], (sent, got), "step", 100_000, 4)
    got = lax.ppermute(sent, "region", cube_pairs(count, 4))
    mine, kernel_part = call(
        spread_kernel, [((peers, LONG, C), BF), ((8, 192), F32)], [], (sent, got),
        "spread", 1_000_000, 8,
    )
    mine = lax.all_to_all(mine, "chan", split_axis=0, concat_axis=0, tiled=True)

    grad_low, grad_high = shifted(grad)
    kernel_part = sum_four(kernel_part, swap, cube_pairs(count, 1), cube_pairs(count, 1, 1))
    kernel_part = kernel_part.reshape(8, 3, 64).transpose(1, 0, 2).reshape(CH, 64)
    kernel_part = kernel_part[:, :49] * factor
    (input_grad,) = call(
        functools.partial(backward_kernel, total_tiles),
        [((ROWS, PIX), BF)],
        [padded, square, taps],
        (region, grad, grad_low, grad_high, neighbours, kernel, upstream),
        "backward_conv",
        400_000_000,
        16,
        smem=(0,),
    )

    mine, kernel_part, input_grad = lax.optimization_barrier((mine, kernel_part, input_grad))
    other = lax.ppermute(mine, "region", swap)
    grads = [((HID, C), F32), ((C, HID), F32)]
    scratch = [((768, C), F32), ((C, 768), F32), ((2,), None)]
    placed = call(
        functools.partial(place_own_kernel, factor),
        grads, scratch, (region, mine), "place_own", 1_000_000, 16, smem=(0,), far=(2, 3),
    )
    grad_weight_in, grad_weight_out = call(
        functools.partial(place_other_kernel, factor),
        grads, scratch, (region, other, *placed), "place_other", 1_000_000, 16,
        smem=(0,), far=(2, 3, 4, 5), aliases={2: 0, 3: 1},
    )

    small = (mine[0, PART:].astype(F32) + other[0, PART:].astype(F32)) * factor
    return (
        output.reshape(features.shape),
        input_grad.reshape(features.shape),
        grad_weight_in,
        grad_weight_out,
        small[0:4].reshape(HID),
        small[4],
        small[5],
        small[6],
        kernel_part,
    )


def solution(mesh):
    block = P("chan", "region", None)
    in_specs = (block, block, P(None, "region"), P("chan", None)) + (P(),) * 6
    out_specs = (block, block) + (P(),) * 6 + (P("chan", None),)
    return jax.shard_map(
        per_device, mesh=mesh, in_specs=in_specs, out_specs=out_specs, check_vma=False
    )
```

```python
import functools
import math

import jax
import jax.numpy as jnp
from jax import lax
from jax.experimental import pallas as pl
from jax.experimental.pallas import tpu as pltpu
from jax.sharding import PartitionSpec as P

TS = 16
CH = 24
TILE = 16
PIX = 256
ROWS = CH * TILE
C = 384
HID = 1536
PART = 96
EXTRA = 8
LONG = PART + EXTRA
BRANCH = 32
F32 = jnp.float32
BF = jnp.bfloat16
NT = (((1,), (1,)), ((), ()))
NN = (((1,), (0,)), ((), ()))
TN = (((0,), (0,)), ((), ()))


def iota(shape, dim):
    return lax.broadcasted_iota(jnp.int32, shape, dim)


def dot(left, right, dims=NN):
    return lax.dot_general(left, right, dims, preferred_element_type=F32)


def eye(n):
    return (iota((n, n), 0) == iota((n, n), 1)).astype(F32).astype(BF)


def tile_major():
    column = iota((ROWS, ROWS), 1)
    target = (column & 15) * CH + (column >> 4)
    return (iota((ROWS, ROWS), 0) == target).astype(F32).astype(BF)


def chan_major():
    row = iota((ROWS, ROWS), 0)
    target = (row & 15) * CH + (row >> 4)
    return (iota((ROWS, ROWS), 1) == target).astype(F32).astype(BF)


def fill_padded(pad, own, low, high, lookup):
    identity = eye(PIX)
    own_t = dot(identity, own, NT)
    own_b = own_t.astype(BF)
    low_b = dot(identity, low, NT).astype(BF)
    high_b = dot(identity, high, NT).astype(BF)
    row = iota((ROWS, 128), 0)
    lane = iota((ROWS, 128), 1)
    key = jnp.where(((row >> 4) & 7) == (lane >> 4), (row >> 7) * 16 + (row & 15), -1)

    def pick(directions):
        parts = [
            (key == lookup[d : d + 1, :]).astype(F32).astype(BF) for d in directions
        ]
        return jnp.concatenate(parts, axis=1)

    north = pick((0, 4, 5))
    south = pick((1, 6, 7))
    sides = pick((2, 3))
    for g in range(3):
        lanes = slice(g * 128, (g + 1) * 128)
        table = jnp.concatenate([low_b[:, lanes], own_b[:, lanes], high_b[:, lanes]], axis=1)
        top = dot(table[208:256], north)
        bottom = dot(table[0:48], south)
        side = dot(table, sides)
        pad[g, 3:19, 3:19, :] = own_t[:, lanes].reshape(16, 16, 128)
        pad[g, 0:3, 3:19, :] = top[:, 0:128].reshape(3, 16, 128)
        pad[g, 0:3, 0:3, :] = top[:, 128:256].reshape(3, 16, 128)[:, 13:16]
        pad[g, 0:3, 19:22, :] = top[:, 256:384].reshape(3, 16, 128)[:, 0:3]
        pad[g, 19:22, 3:19, :] = bottom[:, 0:128].reshape(3, 16, 128)
        pad[g, 19:22, 0:3, :] = bottom[:, 128:256].reshape(3, 16, 128)[:, 13:16]
        pad[g, 19:22, 19:22, :] = bottom[:, 256:384].reshape(3, 16, 128)[:, 0:3]
        pad[g, 3:19, 0:3, :] = side[:, 0:128].reshape(16, 16, 128)[:, 13:16]
        pad[g, 3:19, 19:22, :] = side[:, 128:256].reshape(16, 16, 128)[:, 0:3]


def lookup_rows(region, neighbours, total):
    raw = neighbours[...]
    place = jnp.where(raw >= total, 3 * TILE, raw - (region[0] - 1) * TILE)
    repeat = ((iota((TILE, 128), 1) & 15) == iota((TILE, 128), 0)).astype(F32)
    return dot(place.astype(F32), repeat).astype(jnp.int32)


def spread_taps(kernel, weights):
    member = (iota((CH, ROWS), 0) == (iota((CH, ROWS), 1) >> 4)).astype(F32)
    wide = lax.dot_general(
        kernel[...], member, (((0,), (0,)), ((), ())),
        preferred_element_type=F32, precision=lax.Precision.HIGHEST,
    )
    for g in range(3):
        weights[g] = wide[:, g * 128 : (g + 1) * 128]


def convolve(pad, weights, result, flip):
    def group(g, carry):
        for half in range(2):
            total = [None] * TS
            for b in range(7):
                taps = [
                    weights[g, pl.ds((48 - 7 * a - b) if flip else (7 * a + b), 1), :]
                    for a in range(7)
                ]
                taps = [jnp.broadcast_to(t, (8, 128)) for t in taps]
                for r in range(22):
                    value = pad[g, r, pl.ds(b + 8 * half, 8), :]
                    for a in range(7):
                        i = r - a
                        if 0 <= i < TS:
                            term = taps[a] * value
                            total[i] = term if total[i] is None else total[i] + term
            for i in range(TS):
                result[g, i, pl.ds(8 * half, 8), :] = total[i]
        return carry

    lax.fori_loop(0, 3, group, 0)


def rows_of(result):
    return jnp.concatenate([result[g].reshape(PIX, 128) for g in range(3)], axis=1)


def forward_kernel(
    total, region, own, near, far, neighbours, kernel, cotangent, both, pad_out,
    pad, result, weights, own_ref, sides, neighbours_ref, kernel_ref, cotangent_ref, sems,
):
    core = region[0] & 1
    pairs = [
        (kernel, kernel_ref), (neighbours, neighbours_ref), (own, own_ref),
        (near, sides.at[1 - core]), (far, sides.at[core]), (cotangent, cotangent_ref),
    ]
    loads = [pltpu.make_async_copy(*pair, sems.at[i]) for i, pair in enumerate(pairs)]
    for load in loads:
        load.start()
    order = tile_major()
    loads[0].wait()
    spread_taps(kernel_ref, weights)
    for load in loads[1:5]:
        load.wait()
    lookup = lookup_rows(region, neighbours_ref, total)
    fill_padded(pad, own_ref[...], sides[0], sides[1], lookup)
    store = pltpu.make_async_copy(pad, pad_out, sems.at[6])
    store.start()
    convolve(pad, weights, result, False)
    both[:, :PIX] = dot(order, rows_of(result).astype(BF), NT).astype(BF)
    loads[5].wait()
    both[:, PIX:] = dot(order, cotangent_ref[...]).astype(BF)
    store.wait()


def taps_kernel(
    received, features, pad_x, output, grad, kernel_grad, unpacked, gradient, sums
):
    for t in range(TILE):
        part = received[t, 0:BRANCH, :].astype(F32)
        rows = slice(t * CH, (t + 1) * CH)
        unpacked[rows, 0:384] = part[0:CH]
        for i in range(3):
            piece = part[CH:, i * 128 : (i + 1) * 128]
            unpacked[t * CH + 8 * i : t * CH + 8 * (i + 1), 384:512] = piece
    both = dot(chan_major(), unpacked[...].astype(BF))
    output[...] = (features[...].astype(F32) + both[:, :PIX]).astype(BF)
    own_grad = both[:, PIX:].astype(BF)
    grad[...] = own_grad
    own = dot(eye(PIX), own_grad, NT)
    for g in range(3):
        gradient[g] = own[:, g * 128 : (g + 1) * 128].reshape(TS, TS, 128)
    sums[...] = jnp.zeros_like(sums)

    def group(g, carry):
        for b in range(7):
            total = [None] * 7
            for half in range(2):
                grads = [gradient[g, i, pl.ds(8 * half, 8), :] for i in range(TS)]
                for r in range(22):
                    value = pad_x[g, r, pl.ds(b + 8 * half, 8), :]
                    for a in range(7):
                        i = r - a
                        if 0 <= i < TS:
                            term = grads[i] * value
                            total[a] = term if total[a] is None else total[a] + term
            for a in range(7):
                sums[g, pl.ds(7 * a + b, 1), :] = jnp.sum(total[a], axis=0, keepdims=True)
        return carry

    lax.fori_loop(0, 3, group, 0)
    spread = jnp.concatenate([sums[g] for g in range(3)], axis=1)
    member = (iota((32, ROWS), 0) == (iota((32, ROWS), 1) >> 4)).astype(F32)
    total = lax.dot_general(
        member, spread, NT, preferred_element_type=F32, precision=lax.Precision.HIGHEST
    )
    kernel_grad[...] = halves_of(jnp.concatenate([total[8 * i : 8 * i + 8] for i in range(3)], axis=1))


def halves_of(value):
    high = value.astype(BF).astype(F32)
    return jnp.concatenate([high, value - high], axis=1).astype(BF)


def backward_kernel(
    total_tiles, region, own, near, far, neighbours, kernel, cotangent, input_grad,
    pad, result, weights, sides, sems,
):
    core = region[0] & 1
    loads = [
        pltpu.make_async_copy(near, sides.at[1 - core], sems.at[0]),
        pltpu.make_async_copy(far, sides.at[core], sems.at[1]),
    ]
    for load in loads:
        load.start()
    spread_taps(kernel, weights)
    lookup = lookup_rows(region, neighbours, total_tiles)
    for load in loads:
        load.wait()
    fill_padded(pad, own[...], sides[0], sides[1], lookup)
    convolve(pad, weights, result, True)
    upstream = dot(eye(PIX), cotangent[...], NT)
    total = (upstream + rows_of(result)).astype(BF)
    input_grad[...] = dot(eye(ROWS), total, NT).astype(BF)


def normalize(columns):
    values = columns[:, :PIX].astype(F32)
    centered = values - jnp.mean(values, axis=0, keepdims=True)
    inv_std = lax.rsqrt(jnp.mean(centered * centered, axis=0, keepdims=True) + 1e-06)
    return centered * inv_std, inv_std


def stage_kernel(weight_out, copied):
    copied[...] = weight_out[...]


def hidden_blocks(
    side, table, inputs, grad_mixed, bias, weight_in, weight_out, parts, mixed_out, grad_inputs, small,
):
    lane = iota((C, 128), 1)
    for q in range(4):
        bias[q * C : (q + 1) * C, :] = table[:, q : q + 1]
    for k in range(2):
        block = 2 * side + k
        rows = pl.ds(pl.multiple_of(block * C, C), C)
        hidden = dot(weight_in[rows, :], inputs) + bias[rows, :]
        cdf = 0.5 + 0.5 * lax.erf(hidden * 0.7071067811865476)
        activation = (hidden * cdf).astype(BF)
        slope = cdf + hidden * jnp.exp(-0.5 * hidden * hidden) * 0.3989422804014327
        mixed_out = mixed_out + dot(weight_out[:, rows], activation)
        grad_hidden = dot(weight_out[:, rows], grad_mixed, TN) * slope
        small = small + jnp.where(
            lane == block, jnp.sum(grad_hidden, axis=1, keepdims=True), 0.0
        )
        hidden_grad = grad_hidden.astype(BF)
        grad_inputs = grad_inputs + dot(weight_in[rows, :], hidden_grad, TN)
        part = dot(hidden_grad, inputs, NT).astype(BF)
        for s in range(4):
            parts[4 * k + s] = part[s * PART : (s + 1) * PART]
        part = dot(grad_mixed, activation, NT).astype(BF)
        for s in range(4):
            parts[8 + 4 * k + s] = part[s * PART : (s + 1) * PART]
    return mixed_out, grad_inputs, small


def first_half_kernel(
    region, columns, vectors, weight_in, weight_out,
    parts, mixed_sum, grad_sum, small_sum, bias,
):
    table = jnp.transpose(vectors[...])
    normed, _ = normalize(columns)
    inputs = (normed * table[:, 4:5] + table[:, 5:6]).astype(BF)
    grad_mixed = (table[:, 6:7] * columns[:, PIX:].astype(F32)).astype(BF)
    zeros = jnp.zeros((C, PIX), F32)
    mixed_sum[...], grad_sum[...], small_sum[...] = hidden_blocks(
        1 - (region[0] & 1), table, inputs, grad_mixed, bias,
        weight_in, weight_out, parts, zeros, zeros, jnp.zeros((C, 128), F32),
    )


def second_half_kernel(
    region, columns, vectors, weight_in, weight_out,
    mixed_sum, grad_sum, small_sum, out, parts, extra, bias,
):
    table = jnp.transpose(vectors[...])
    gain = table[:, 4:5]
    scale = table[:, 6:7]
    normed, inv_std = normalize(columns)
    inputs = (normed * gain + table[:, 5:6]).astype(BF)
    upstream = columns[:, PIX:].astype(F32)
    grad_mixed = (scale * upstream).astype(BF)
    mixed_out, grad_inputs, small = hidden_blocks(
        region[0] & 1, table, inputs, grad_mixed, bias,
        weight_in, weight_out, parts, mixed_sum[...], grad_sum[...], small_sum[...],
    )
    branch = scale * mixed_out
    grad_scale = jnp.sum(upstream * mixed_out, axis=1, keepdims=True)
    grad_gain = jnp.sum(grad_inputs * normed, axis=1, keepdims=True)
    grad_shift = jnp.sum(grad_inputs, axis=1, keepdims=True)
    grad_normed = grad_inputs * gain
    grad_conv = (
        grad_normed
        - jnp.mean(grad_normed, axis=0, keepdims=True)
        - normed * jnp.mean(grad_normed * normed, axis=0, keepdims=True)
    ) * inv_std
    for j in range(16):
        rows = slice(j * CH, (j + 1) * CH)
        side = grad_conv[rows, 128:]
        first = jnp.concatenate([branch[rows], grad_conv[rows, :128]], axis=1)
        last = jnp.concatenate([side[8 * i : 8 * i + 8] for i in range(3)], axis=1)
        out[j] = jnp.concatenate([first, last], axis=0).astype(BF)
    lane = iota((C, 128), 1)
    small = small + jnp.where(lane == 4, grad_gain, 0.0)
    small = small + jnp.where(lane == 5, grad_shift, 0.0)
    small = small + jnp.where(lane == 6, grad_scale, 0.0)
    extra[...] = jnp.transpose(small)[0:EXTRA].astype(BF)


def add_kernel(out, first, second, extra, total):
    total[:, 0:BRANCH, :] = out[...]
    total[:, BRANCH : BRANCH + PART, :] = (
        first[...].astype(F32) + second[...].astype(F32)
    ).astype(BF)
    total[0, BRANCH + PART :, :] = extra[...]
    total[1:, BRANCH + PART :, :] = jnp.zeros((15, EXTRA, C), BF)


def first_step_kernel(sent, got, kernel_grad, total):
    total[0:LONG, :] = (sent[...].astype(F32) + got[...].astype(F32)).astype(BF)
    total[LONG:, :] = kernel_grad[...]


def joined(sent, got):
    value = sent[...].astype(F32) + got[...].astype(F32)
    return value[0:LONG].astype(BF), value[LONG:, :192] + value[LONG:, 192:]


def next_step_kernel(sent, got, total):
    weights, taps = joined(sent, got)
    total[0:LONG, :] = weights
    total[LONG:, :] = halves_of(taps)


def spread_kernel(sent, got, total, kernel_grad, value, sems):
    value[...], kernel_grad[...] = joined(sent, got)
    stores = [pltpu.make_async_copy(value, total.at[j], sems.at[j]) for j in range(16)]
    for store in stores:
        store.start()
    for store in stores:
        store.wait()


def place(factor, side, ref, grad_in, grad_out, tall, wide, sems):
    half = pl.multiple_of(side * 768, 768)
    stores = []
    for j in range(8):
        rows = pl.ds(j * PART, PART)
        tall[rows, :] = ref[j, 0:PART, :].astype(F32) * factor
        target = grad_in.at[pl.ds(half + j * PART, PART), :]
        stores.append(pltpu.make_async_copy(tall.at[rows, :], target, sems.at[j]))
        stores[-1].start()
    for s in range(4):
        rows = pl.ds(s * PART, PART)
        for k in range(2):
            wide[rows, k * C : (k + 1) * C] = ref[8 + 4 * k + s, 0:PART, :].astype(F32) * factor
        target = grad_out.at[rows, pl.ds(half, 768)]
        stores.append(pltpu.make_async_copy(wide.at[rows, :], target, sems.at[8 + s]))
        stores[-1].start()
    return stores


def place_own_kernel(factor, region, ref, grad_in, grad_out, tall, wide, sems):
    for store in place(factor, region[0] & 1, ref, grad_in, grad_out, tall, wide, sems):
        store.wait()


def place_other_kernel(
    factor, region, ref, in_a, out_a, own_extra, grad_in, grad_out, bias, gain, shift, scale,
    tall, wide, sems,
):
    stores = place(factor, 1 - (region[0] & 1), ref, grad_in, grad_out, tall, wide, sems)
    small = (own_extra[...].astype(F32) + ref[0, PART:, :].astype(F32)) * factor
    for q in range(4):
        bias[q * C : (q + 1) * C] = small[q]
    gain[...] = small[4]
    shift[...] = small[5]
    scale[...] = small[6]
    for store in stores:
        store.wait()


def call(
    body, shapes, scratch, args, name, flops, limit, smem=(), far=(), anywhere=(), aliases=None
):
    spaces = [pltpu.VMEM] * (len(args) + len(shapes))
    for space, places in ((pltpu.SMEM, smem), (pltpu.HBM, far), (pl.ANY, anywhere)):
        for i in places:
            spaces[i] = space
    spaces = [pl.BlockSpec(memory_space=space) for space in spaces]
    moved = sum(a.size * a.dtype.itemsize for a in args)
    moved += sum(math.prod(s) * jnp.dtype(d).itemsize for s, d in shapes)
    return pl.pallas_call(
        body,
        out_shape=[jax.ShapeDtypeStruct(s, d) for s, d in shapes],
        in_specs=spaces[: len(args)],
        out_specs=spaces[len(args) :],
        scratch_shapes=[
            pltpu.SemaphoreType.DMA(s) if d is None else pltpu.VMEM(s, d) for s, d in scratch
        ],
        compiler_params=pltpu.CompilerParams(vmem_limit_bytes=limit * 1024 * 1024),
        cost_estimate=pl.CostEstimate(flops=flops, bytes_accessed=moved, transcendentals=0),
        input_output_aliases=aliases or {},
        name=name,
    )(*args)


def both_sides(field):
    count = lax.axis_size("region")
    near = [(i, i ^ 1) for i in range(count)]
    far = [(i, ((i + 1) ^ 1) - 1) for i in range(1, count - 1)]
    return lax.ppermute(field, "region", near), lax.ppermute(field, "region", far)


def cube_pairs(count, bit, core=0):
    ring = count // 2
    label = [z ^ (z >> 1) for z in range(ring)]
    place = {g: z for z, g in enumerate(label)}
    return [
        (2 * z + c, 2 * place[label[z] ^ bit] + (c ^ core)) for z in range(ring) for c in range(2)
    ]


def sum_four(value, first, second, both):
    near, far, across = (lax.ppermute(value, "region", pairs) for pairs in (first, second, both))
    return (value + near) + (far + across)


def per_device(
    features, cotangent, neighbours, kernel, norm_gain, norm_shift,
    weight_in, bias_in, weight_out, layer_scale,
):
    count = lax.axis_size("region")
    peers = lax.axis_size("chan")
    region = lax.axis_index("region").astype(jnp.int32).reshape(1)
    total_tiles = TILE * count
    factor = 1.0 / math.sqrt(total_tiles * PIX)
    swap = [(i, i ^ 1) for i in range(count)]

    x = features.reshape(ROWS, PIX)
    upstream = cotangent.reshape(ROWS, PIX)
    x_near, x_far = both_sides(x)
    vectors = jnp.concatenate(
        [
            bias_in.reshape(4, C), norm_gain[None], norm_shift[None], layer_scale[None],
            jnp.zeros((1, C), F32),
        ],
        axis=0,
    )

    padded = ((3, 22, 24, 128), F32)
    square = ((3, 16, 16, 128), F32)
    taps = ((3, 49, 128), F32)
    block = ((ROWS, PIX), BF)
    pair = ((2, ROWS, PIX), BF)
    columns, pad_x = call(
        functools.partial(forward_kernel, total_tiles),
        [((ROWS, 2 * PIX), BF), padded],
        [
            padded, square, taps, block, pair, ((8, TILE), jnp.int32), ((CH, 49), F32),
            block, ((7,), None),
        ],
        (region, x, x_near, x_far, neighbours, kernel, upstream),
        "forward_conv",
        400_000_000,
        56,
        smem=(0,),
        far=(1, 4, 5, 6, 8),
        anywhere=(2, 3),
    )
    columns = lax.all_to_all(columns, "chan", split_axis=0, concat_axis=0, tiled=True)

    (staged,) = call(stage_kernel, [((C, HID), BF)], [], (weight_out,), "stage", 1_000_000, 6)
    halves = (16, PART, C)
    pixels = (region, columns, vectors, weight_in, staged)
    scratch = [((HID, 1), F32)]
    sums = [((C, PIX), F32), ((C, PIX), F32), ((C, 128), F32)]
    send, *partial = call(
        first_half_kernel,
        [(halves, BF)] + sums,
        scratch,
        pixels,
        "pixels_first",
        1_000_000_000,
        24,
        smem=(0,),
    )
    partner = lax.ppermute(send, "region", swap)
    out, keep, extra = call(
        second_half_kernel,
        [((16, BRANCH, C), BF), (halves, BF), ((EXTRA, C), BF)],
        scratch,
        (*pixels, *partial),
        "pixels_second",
        1_000_000_000,
        24,
        smem=(0,),
    )
    (travel,) = call(
        add_kernel, [((16, BRANCH + LONG, C), BF)], [], (out, keep, partner, extra),
        "add_cores", 1_000_000, 8,
    )
    travel = lax.all_to_all(travel, "chan", split_axis=0, concat_axis=0, tiled=True)

    sent = jnp.sum(travel[:, BRANCH:].astype(F32), axis=0).astype(BF)
    got = lax.ppermute(sent, "region", cube_pairs(count, 1))
    output, grad, kernel_part = call(
        taps_kernel,
        [((ROWS, PIX), BF), ((ROWS, PIX), BF), ((8, C), BF)],
        [((ROWS, 2 * PIX), F32), square, ((3, 64, 128), F32)],
        (travel, x, pad_x),
        "kernel_taps",
        400_000_000,
        16,
    )
    step = [((LONG + 8, C), BF)]
    (sent,) = call(first_step_kernel, step, [], (sent, got, kernel_part), "step", 100_000, 4)
    got = lax.ppermute(sent, "region", cube_pairs(count, 2))
    (sent,) = call(next_step_kernel, step, [], (sent, got), "step", 100_000, 4)
    got = lax.ppermute(sent, "region", cube_pairs(count, 4))
    mine, kernel_part = call(
        spread_kernel, [((peers, LONG, C), BF), ((8, 192), F32)],
        [((LONG, C), BF), ((16,), None)], (sent, got), "spread", 1_000_000, 8, far=(2,),
    )
    mine = lax.all_to_all(mine, "chan", split_axis=0, concat_axis=0, tiled=True)

    grad_near, grad_far = both_sides(grad)
    kernel_part = sum_four(kernel_part, swap, cube_pairs(count, 1), cube_pairs(count, 1, 1))
    kernel_part = kernel_part.reshape(8, 3, 64).transpose(1, 0, 2).reshape(CH, 64)
    kernel_part = kernel_part[:, :49] * factor
    (input_grad,) = call(
        functools.partial(backward_kernel, total_tiles),
        [((ROWS, PIX), BF)],
        [padded, square, taps, pair, ((2,), None)],
        (region, grad, grad_near, grad_far, neighbours, kernel, upstream),
        "backward_conv",
        400_000_000,
        16,
        smem=(0,),
        anywhere=(2, 3),
    )

    mine, kernel_part, input_grad = lax.optimization_barrier((mine, kernel_part, input_grad))
    other = lax.ppermute(mine, "region", swap)
    grads = [((HID, C), F32), ((C, HID), F32)]
    scratch = [((768, C), F32), ((C, 768), F32), ((12,), None)]
    placed = call(
        functools.partial(place_own_kernel, factor),
        grads, scratch, (region, mine), "place_own", 1_000_000, 16, smem=(0,), far=(2, 3),
    )
    vector = ((C,), F32)
    grad_weight_in, grad_weight_out, grad_bias, grad_gain, grad_shift, grad_scale = call(
        functools.partial(place_other_kernel, factor),
        grads + [((HID,), F32), vector, vector, vector],
        scratch, (region, other, *placed, mine[0, PART:]), "place_other", 1_000_000, 16,
        smem=(0,), far=(2, 3, 5, 6), aliases={2: 0, 3: 1},
    )
    return (
        output.reshape(features.shape),
        input_grad.reshape(features.shape),
        grad_weight_in,
        grad_weight_out,
        grad_bias,
        grad_gain,
        grad_shift,
        grad_scale,
        kernel_part,
    )


def solution(mesh):
    block = P("chan", "region", None)
    in_specs = (block, block, P(None, "region"), P("chan", None)) + (P(),) * 6
    out_specs = (block, block) + (P(),) * 6 + (P("chan", None),)
    return jax.shard_map(
        per_device, mesh=mesh, in_specs=in_specs, out_specs=out_specs, check_vma=False
    )
```

```python
import functools
import math

import jax
import jax.numpy as jnp
from jax import lax
from jax.experimental import pallas as pl
from jax.experimental.pallas import tpu as pltpu
from jax.sharding import PartitionSpec as P

TS = 16
CH = 24
TILE = 16
PIX = 256
ROWS = CH * TILE
C = 384
HID = 1536
PART = 96
EXTRA = 8
LONG = PART + EXTRA
BRANCH = 32
F32 = jnp.float32
BF = jnp.bfloat16
NT = (((1,), (1,)), ((), ()))
NN = (((1,), (0,)), ((), ()))
TN = (((0,), (0,)), ((), ()))


def iota(shape, dim):
    return lax.broadcasted_iota(jnp.int32, shape, dim)


def dot(left, right, dims=NN):
    return lax.dot_general(left, right, dims, preferred_element_type=F32)


def eye(n):
    return (iota((n, n), 0) == iota((n, n), 1)).astype(F32).astype(BF)


def tile_major():
    column = iota((ROWS, ROWS), 1)
    target = (column & 15) * CH + (column >> 4)
    return (iota((ROWS, ROWS), 0) == target).astype(F32).astype(BF)


def chan_major():
    row = iota((ROWS, ROWS), 0)
    target = (row & 15) * CH + (row >> 4)
    return (iota((ROWS, ROWS), 1) == target).astype(F32).astype(BF)


def one_hots(lookup):
    row = iota((ROWS, 128), 0)
    lane = iota((ROWS, 128), 1)
    key = jnp.where(((row >> 4) & 7) == (lane >> 4), (row >> 7) * 16 + (row & 15), -1)
    parts = [
        (key == lookup[d : d + 1, :]).astype(F32).astype(BF) for d in (0, 4, 5, 1, 6, 7, 2, 3)
    ]
    return jnp.concatenate(parts, axis=1)


def fill_padded(pad, own, low, high, picks):
    for g in range(3):
        lanes = slice(g * 128, (g + 1) * 128)
        table = jnp.concatenate([low[:, lanes], own[:, lanes], high[:, lanes]], axis=1)
        top = dot(table[208:256], picks[:, 0:384])
        bottom = dot(table[0:48], picks[:, 384:768])
        side = dot(table, picks[:, 768:1024])
        pad[g, 3:19, 3:19, :] = own[:, lanes].astype(F32).reshape(16, 16, 128)
        pad[g, 0:3, 3:19, :] = top[:, 0:128].reshape(3, 16, 128)
        pad[g, 0:3, 0:3, :] = top[:, 128:256].reshape(3, 16, 128)[:, 13:16]
        pad[g, 0:3, 19:22, :] = top[:, 256:384].reshape(3, 16, 128)[:, 0:3]
        pad[g, 19:22, 3:19, :] = bottom[:, 0:128].reshape(3, 16, 128)
        pad[g, 19:22, 0:3, :] = bottom[:, 128:256].reshape(3, 16, 128)[:, 13:16]
        pad[g, 19:22, 19:22, :] = bottom[:, 256:384].reshape(3, 16, 128)[:, 0:3]
        pad[g, 3:19, 0:3, :] = side[:, 0:128].reshape(16, 16, 128)[:, 13:16]
        pad[g, 3:19, 19:22, :] = side[:, 128:256].reshape(16, 16, 128)[:, 0:3]


def lookup_rows(region, neighbours, total):
    raw = neighbours[...]
    place = jnp.where(raw >= total, 3 * TILE, raw - (region[0] - 1) * TILE)
    repeat = ((iota((TILE, 128), 1) & 15) == iota((TILE, 128), 0)).astype(F32)
    return dot(place.astype(F32), repeat).astype(jnp.int32)


def spread_taps(kernel, weights):
    member = (iota((CH, ROWS), 0) == (iota((CH, ROWS), 1) >> 4)).astype(F32)
    wide = lax.dot_general(
        kernel, member, TN, preferred_element_type=F32, precision=lax.Precision.HIGHEST
    )
    for g in range(3):
        weights[g] = wide[:, g * 128 : (g + 1) * 128]


def convolve(pad, weights, result, flip):
    def group(g, carry):
        for half in range(2):
            total = [None] * TS
            for b in range(7):
                taps = [
                    weights[g, pl.ds((48 - 7 * a - b) if flip else (7 * a + b), 1), :]
                    for a in range(7)
                ]
                taps = [jnp.broadcast_to(t, (8, 128)) for t in taps]
                for r in range(22):
                    value = pad[g, r, pl.ds(b + 8 * half, 8), :]
                    for a in range(7):
                        i = r - a
                        if 0 <= i < TS:
                            term = taps[a] * value
                            total[i] = term if total[i] is None else total[i] + term
            for i in range(TS):
                result[g, i, pl.ds(8 * half, 8), :] = total[i]
        return carry

    lax.fori_loop(0, 3, group, 0)


def rows_of(result):
    return jnp.concatenate([result[g].reshape(PIX, 128) for g in range(3)], axis=1)


def prepare_kernel(
    total, region, neighbours, own, kernel, cotangent, own_t, upstream, weights, picks, order
):
    spread_taps(kernel[...], weights)
    picks[...] = one_hots(lookup_rows(region, neighbours, total))
    order[...] = tile_major()
    own_t[...] = dot(eye(PIX), own[...], NT).astype(BF)
    upstream[...] = dot(order[...], cotangent[...]).astype(BF)


def sides_of(region, near, far):
    first = region[0] & 1 == 0
    near_t = dot(eye(PIX), near[...], NT)
    far_t = dot(eye(PIX), far[...], NT)
    low = jnp.where(first, far_t, near_t).astype(BF)
    high = jnp.where(first, near_t, far_t).astype(BF)
    return low, high


def forward_kernel(
    region, near, far, own_t, upstream, weights, picks, order, both, pad_out,
    pad, result, conv, sems,
):
    stores = [pltpu.make_async_copy(upstream, both.at[:, pl.ds(PIX, PIX)], sems.at[0])]
    stores[0].start()
    fill_padded(pad, own_t[...], *sides_of(region, near, far), picks)
    pad_out[...] = pad[...].astype(BF)
    convolve(pad, weights, result, False)
    conv[...] = dot(order[...], rows_of(result).astype(BF), NT).astype(BF)
    stores.append(pltpu.make_async_copy(conv, both.at[:, pl.ds(0, PIX)], sems.at[1]))
    stores[1].start()
    for store in stores:
        store.wait()


def taps_kernel(
    received, features, pad_x, output, grad, kernel_grad, unpacked, gradient, sums, pad
):
    for t in range(TILE):
        part = received[t, 0:BRANCH, :].astype(F32)
        rows = slice(t * CH, (t + 1) * CH)
        unpacked[rows, 0:384] = part[0:CH]
        for i in range(3):
            piece = part[CH:, i * 128 : (i + 1) * 128]
            unpacked[t * CH + 8 * i : t * CH + 8 * (i + 1), 384:512] = piece
    both = dot(chan_major(), unpacked[...].astype(BF))
    output[...] = (features[...].astype(F32) + both[:, :PIX]).astype(BF)
    own_grad = both[:, PIX:].astype(BF)
    grad[...] = own_grad
    own = dot(eye(PIX), own_grad, NT)
    for g in range(3):
        gradient[g] = own[:, g * 128 : (g + 1) * 128].reshape(TS, TS, 128)
    sums[...] = jnp.zeros_like(sums)
    pad[...] = pad_x[...].astype(F32)

    def group(g, carry):
        for b in range(7):
            total = [None] * 7
            for half in range(2):
                grads = [gradient[g, i, pl.ds(8 * half, 8), :] for i in range(TS)]
                for r in range(22):
                    value = pad[g, r, pl.ds(b + 8 * half, 8), :]
                    for a in range(7):
                        i = r - a
                        if 0 <= i < TS:
                            term = grads[i] * value
                            total[a] = term if total[a] is None else total[a] + term
            for a in range(7):
                sums[g, pl.ds(7 * a + b, 1), :] = jnp.sum(total[a], axis=0, keepdims=True)
        return carry

    lax.fori_loop(0, 3, group, 0)
    spread = jnp.concatenate([sums[g] for g in range(3)], axis=1)
    member = (iota((32, ROWS), 0) == (iota((32, ROWS), 1) >> 4)).astype(F32)
    total = lax.dot_general(
        member, spread, NT, preferred_element_type=F32, precision=lax.Precision.HIGHEST
    )
    kernel_grad[...] = halves_of(jnp.concatenate([total[8 * i : 8 * i + 8] for i in range(3)], axis=1))


def halves_of(value):
    high = value.astype(BF).astype(F32)
    return jnp.concatenate([high, value - high], axis=1).astype(BF)


def backward_kernel(
    total, region, neighbours, own, near, far, kernel, cotangent, input_grad,
    pad, result, weights, picks,
):
    spread_taps(kernel[...], weights)
    picks[...] = one_hots(lookup_rows(region, neighbours, total))
    own_t = dot(eye(PIX), own[...], NT).astype(BF)
    fill_padded(pad, own_t, *sides_of(region, near, far), picks)
    convolve(pad, weights, result, True)
    upstream = dot(eye(PIX), cotangent[...], NT)
    total = (upstream + rows_of(result)).astype(BF)
    input_grad[...] = dot(eye(ROWS), total, NT).astype(BF)


def normalize(columns):
    values = columns[:, :PIX].astype(F32)
    centered = values - jnp.mean(values, axis=0, keepdims=True)
    inv_std = lax.rsqrt(jnp.mean(centered * centered, axis=0, keepdims=True) + 1e-06)
    return centered * inv_std, inv_std


def stage_kernel(weight_in, weight_out, both):
    both[0:HID, :] = weight_in[...]
    for q in range(4):
        both[HID + q * C : HID + (q + 1) * C, :] = weight_out[:, q * C : (q + 1) * C]


def hidden_blocks(
    side, table, inputs, grad_mixed, bias, matrices, parts, mixed_out, grad_inputs, small,
):
    lane = iota((C, 128), 1)
    for q in range(4):
        bias[q * C : (q + 1) * C, :] = table[:, q : q + 1]
    for k in range(2):
        block = 2 * side + k
        rows = pl.ds(pl.multiple_of(block * C, C), C)
        weight_in = matrices[rows, :]
        weight_out = matrices[pl.ds(pl.multiple_of(HID + block * C, C), C), :]
        hidden = dot(weight_in, inputs) + bias[rows, :]
        cdf = 0.5 + 0.5 * lax.erf(hidden * 0.7071067811865476)
        activation = (hidden * cdf).astype(BF)
        slope = cdf + hidden * jnp.exp(-0.5 * hidden * hidden) * 0.3989422804014327
        mixed_out = mixed_out + dot(weight_out, activation)
        grad_hidden = dot(weight_out, grad_mixed, TN) * slope
        small = small + jnp.where(
            lane == block, jnp.sum(grad_hidden, axis=1, keepdims=True), 0.0
        )
        hidden_grad = grad_hidden.astype(BF)
        grad_inputs = grad_inputs + dot(weight_in, hidden_grad, TN)
        part = dot(hidden_grad, inputs, NT).astype(BF)
        for s in range(4):
            parts[4 * k + s] = part[s * PART : (s + 1) * PART]
        part = dot(grad_mixed, activation, NT).astype(BF)
        for s in range(4):
            parts[8 + 4 * k + s] = part[s * PART : (s + 1) * PART]
    return mixed_out, grad_inputs, small


def first_half_kernel(
    region, columns, vectors, matrices,
    parts, mixed_sum, grad_sum, small_sum, bias,
):
    table = jnp.transpose(vectors[...])
    normed, _ = normalize(columns)
    inputs = (normed * table[:, 4:5] + table[:, 5:6]).astype(BF)
    grad_mixed = (table[:, 6:7] * columns[:, PIX:].astype(F32)).astype(BF)
    zeros = jnp.zeros((C, PIX), F32)
    mixed_sum[...], grad_sum[...], small_sum[...] = hidden_blocks(
        1 - (region[0] & 1), table, inputs, grad_mixed, bias,
        matrices, parts, zeros, zeros, jnp.zeros((C, 128), F32),
    )


def second_half_kernel(
    region, columns, vectors, matrices,
    mixed_sum, grad_sum, small_sum, out, parts, extra, bias,
):
    table = jnp.transpose(vectors[...])
    gain = table[:, 4:5]
    scale = table[:, 6:7]
    normed, inv_std = normalize(columns)
    inputs = (normed * gain + table[:, 5:6]).astype(BF)
    upstream = columns[:, PIX:].astype(F32)
    grad_mixed = (scale * upstream).astype(BF)
    mixed_out, grad_inputs, small = hidden_blocks(
        region[0] & 1, table, inputs, grad_mixed, bias,
        matrices, parts, mixed_sum[...], grad_sum[...], small_sum[...],
    )
    branch = scale * mixed_out
    grad_scale = jnp.sum(upstream * mixed_out, axis=1, keepdims=True)
    grad_gain = jnp.sum(grad_inputs * normed, axis=1, keepdims=True)
    grad_shift = jnp.sum(grad_inputs, axis=1, keepdims=True)
    grad_normed = grad_inputs * gain
    grad_conv = (
        grad_normed
        - jnp.mean(grad_normed, axis=0, keepdims=True)
        - normed * jnp.mean(grad_normed * normed, axis=0, keepdims=True)
    ) * inv_std
    for j in range(16):
        rows = slice(j * CH, (j + 1) * CH)
        side = grad_conv[rows, 128:]
        first = jnp.concatenate([branch[rows], grad_conv[rows, :128]], axis=1)
        last = jnp.concatenate([side[8 * i : 8 * i + 8] for i in range(3)], axis=1)
        out[j] = jnp.concatenate([first, last], axis=0).astype(BF)
    lane = iota((C, 128), 1)
    small = small + jnp.where(lane == 4, grad_gain, 0.0)
    small = small + jnp.where(lane == 5, grad_shift, 0.0)
    small = small + jnp.where(lane == 6, grad_scale, 0.0)
    extra[...] = jnp.transpose(small)[0:EXTRA].astype(BF)


def add_kernel(out, first, second, extra, total):
    total[:, 0:BRANCH, :] = out[...]
    total[:, BRANCH : BRANCH + PART, :] = (
        first[...].astype(F32) + second[...].astype(F32)
    ).astype(BF)
    total[0, BRANCH + PART :, :] = extra[...]
    total[1:, BRANCH + PART :, :] = jnp.zeros((15, EXTRA, C), BF)


def first_step_kernel(sent, got, kernel_grad, total):
    total[0:LONG, :] = (sent[...].astype(F32) + got[...].astype(F32)).astype(BF)
    total[LONG:, :] = kernel_grad[...]


def joined(sent, got):
    value = sent[...].astype(F32) + got[...].astype(F32)
    return value[0:LONG].astype(BF), value[LONG:, :192] + value[LONG:, 192:]


def next_step_kernel(sent, got, total):
    weights, taps = joined(sent, got)
    total[0:LONG, :] = weights
    total[LONG:, :] = halves_of(taps)


def spread_kernel(sent, got, total, kernel_grad, value, sems):
    value[...], kernel_grad[...] = joined(sent, got)
    stores = [pltpu.make_async_copy(value, total.at[j], sems.at[j]) for j in range(16)]
    for store in stores:
        store.start()
    for store in stores:
        store.wait()


def place(factor, side, ref, grad_in, grad_out, tall, wide, sems):
    half = pl.multiple_of(side * 768, 768)
    stores = []
    for j in range(8):
        rows = pl.ds(j * PART, PART)
        tall[rows, :] = ref[j, 0:PART, :].astype(F32) * factor
        target = grad_in.at[pl.ds(half + j * PART, PART), :]
        stores.append(pltpu.make_async_copy(tall.at[rows, :], target, sems.at[j]))
        stores[-1].start()
    for s in range(4):
        rows = pl.ds(s * PART, PART)
        for k in range(2):
            wide[rows, k * C : (k + 1) * C] = ref[8 + 4 * k + s, 0:PART, :].astype(F32) * factor
        target = grad_out.at[rows, pl.ds(half, 768)]
        stores.append(pltpu.make_async_copy(wide.at[rows, :], target, sems.at[8 + s]))
        stores[-1].start()
    return stores


def place_own_kernel(factor, region, ref, grad_in, grad_out, tall, wide, sems):
    for store in place(factor, region[0] & 1, ref, grad_in, grad_out, tall, wide, sems):
        store.wait()


def place_other_kernel(
    factor, region, ref, in_a, out_a, own_extra, grad_in, grad_out, bias, gain, shift, scale,
    tall, wide, bias_ref, gain_ref, shift_ref, scale_ref, sems,
):
    stores = place(factor, 1 - (region[0] & 1), ref, grad_in, grad_out, tall, wide, sems)
    small = (own_extra[...].astype(F32) + ref[0, PART:, :].astype(F32)) * factor
    for q in range(4):
        bias_ref[q * C : (q + 1) * C] = small[q]
    gain_ref[...] = small[4]
    shift_ref[...] = small[5]
    scale_ref[...] = small[6]
    pairs = [(bias_ref, bias), (gain_ref, gain), (shift_ref, shift), (scale_ref, scale)]
    for i, pair in enumerate(pairs):
        stores.append(pltpu.make_async_copy(*pair, sems.at[12 + i]))
        stores[-1].start()
    for store in stores:
        store.wait()


def call(
    body, shapes, scratch, args, name, flops, limit, smem=(), far=(), anywhere=(), aliases=None
):
    spaces = [pltpu.VMEM] * (len(args) + len(shapes))
    for space, places in ((pltpu.SMEM, smem), (pltpu.HBM, far), (pl.ANY, anywhere)):
        for i in places:
            spaces[i] = space
    spaces = [pl.BlockSpec(memory_space=space) for space in spaces]
    moved = sum(a.size * a.dtype.itemsize for a in args)
    moved += sum(math.prod(s) * jnp.dtype(d).itemsize for s, d in shapes)
    return pl.pallas_call(
        body,
        out_shape=[jax.ShapeDtypeStruct(s, d) for s, d in shapes],
        in_specs=spaces[: len(args)],
        out_specs=spaces[len(args) :],
        scratch_shapes=[
            pltpu.SemaphoreType.DMA(s) if d is None else pltpu.VMEM(s, d) for s, d in scratch
        ],
        compiler_params=pltpu.CompilerParams(vmem_limit_bytes=int(limit * 1024 * 1024)),
        cost_estimate=pl.CostEstimate(flops=flops, bytes_accessed=moved, transcendentals=0),
        input_output_aliases=aliases or {},
        name=name,
    )(*args)


def both_sides(field):
    count = lax.axis_size("region")
    near = [(i, i ^ 1) for i in range(count)]
    far = [(i, ((i + 1) ^ 1) - 1) for i in range(1, count - 1)]
    return lax.ppermute(field, "region", near), lax.ppermute(field, "region", far)


def cube_pairs(count, bit, core=0):
    ring = count // 2
    label = [z ^ (z >> 1) for z in range(ring)]
    place = {g: z for z, g in enumerate(label)}
    return [
        (2 * z + c, 2 * place[label[z] ^ bit] + (c ^ core)) for z in range(ring) for c in range(2)
    ]


def sum_four(value, first, second, both):
    near, far, across = (lax.ppermute(value, "region", pairs) for pairs in (first, second, both))
    return (value + near) + (far + across)


def per_device(
    features, cotangent, neighbours, kernel, norm_gain, norm_shift,
    weight_in, bias_in, weight_out, layer_scale,
):
    count = lax.axis_size("region")
    peers = lax.axis_size("chan")
    region = lax.axis_index("region").astype(jnp.int32).reshape(1)
    total_tiles = TILE * count
    factor = 1.0 / math.sqrt(total_tiles * PIX)
    swap = [(i, i ^ 1) for i in range(count)]

    x = features.reshape(ROWS, PIX)
    upstream = cotangent.reshape(ROWS, PIX)
    x_near, x_far = both_sides(x)
    vectors = jnp.concatenate(
        [
            bias_in.reshape(4, C), norm_gain[None], norm_shift[None], layer_scale[None],
            jnp.zeros((1, C), F32),
        ],
        axis=0,
    )

    padded = ((3, 22, 24, 128), F32)
    square = ((3, 16, 16, 128), F32)
    taps = ((3, 49, 128), F32)
    block = ((ROWS, PIX), BF)
    ready = call(
        functools.partial(prepare_kernel, total_tiles),
        [((PIX, ROWS), BF), block, taps, ((ROWS, 1024), BF), ((ROWS, ROWS), BF)],
        [],
        (region, neighbours, x, kernel, upstream),
        "prepare",
        200_000_000,
        16,
        smem=(0,),
    )
    columns, pad_x = call(
        forward_kernel,
        [((ROWS, 2 * PIX), BF), (padded[0], BF)],
        [padded, square, block, ((2,), None)],
        (region, x_near, x_far, *ready),
        "forward_conv",
        400_000_000,
        16,
        smem=(0,),
        far=(8,),
    )
    columns = lax.all_to_all(columns, "chan", split_axis=0, concat_axis=0, tiled=True)

    staged = call(
        stage_kernel, [((2 * HID, C), BF)], [], (weight_in, weight_out),
        "stage", 1_000_000, 8,
    )
    halves = (16, PART, C)
    pixels = (region, columns, vectors, *staged)
    scratch = [((HID, 1), F32)]
    sums = [((C, PIX), F32), ((C, PIX), F32), ((C, 128), F32)]
    send, *partial = call(
        first_half_kernel,
        [(halves, BF)] + sums,
        scratch,
        pixels,
        "pixels_first",
        1_000_000_000,
        24,
        smem=(0,),
    )
    partner = lax.ppermute(send, "region", swap)
    out, keep, extra = call(
        second_half_kernel,
        [((16, BRANCH, C), BF), (halves, BF), ((EXTRA, C), BF)],
        scratch,
        (*pixels, *partial),
        "pixels_second",
        1_000_000_000,
        24,
        smem=(0,),
    )
    (travel,) = call(
        add_kernel, [((16, BRANCH + LONG, C), BF)], [], (out, keep, partner, extra),
        "add_cores", 1_000_000, 8,
    )
    travel = lax.all_to_all(travel, "chan", split_axis=0, concat_axis=0, tiled=True)

    sent = jnp.sum(travel[:, BRANCH:].astype(F32), axis=0).astype(BF)
    got = lax.ppermute(sent, "region", cube_pairs(count, 1))
    output, grad, kernel_part = call(
        taps_kernel,
        [((ROWS, PIX), BF), ((ROWS, PIX), BF), ((8, C), BF)],
        [((ROWS, 2 * PIX), F32), square, ((3, 64, 128), F32), padded],
        (travel, x, pad_x),
        "kernel_taps",
        400_000_000,
        16,
    )
    step = [((LONG + 8, C), BF)]
    (sent,) = call(first_step_kernel, step, [], (sent, got, kernel_part), "step", 100_000, 4)
    got = lax.ppermute(sent, "region", cube_pairs(count, 2))
    (sent,) = call(next_step_kernel, step, [], (sent, got), "step", 100_000, 4)
    got = lax.ppermute(sent, "region", cube_pairs(count, 4))
    mine, kernel_part = call(
        spread_kernel, [((peers, LONG, C), BF), ((8, 192), F32)],
        [((LONG, C), BF), ((16,), None)], (sent, got), "spread", 1_000_000, 8, far=(2,),
    )
    mine = lax.all_to_all(mine, "chan", split_axis=0, concat_axis=0, tiled=True)

    grad_near, grad_far = both_sides(grad)
    kernel_part = sum_four(kernel_part, swap, cube_pairs(count, 1), cube_pairs(count, 1, 1))
    kernel_part = kernel_part.reshape(8, 3, 64).transpose(1, 0, 2).reshape(CH, 64)
    kernel_part = kernel_part[:, :49] * factor
    (input_grad,) = call(
        functools.partial(backward_kernel, total_tiles),
        [block],
        [padded, square, taps, ((ROWS, 1024), BF)],
        (region, neighbours, grad, grad_near, grad_far, kernel, upstream),
        "backward_conv",
        400_000_000,
        16,
        smem=(0,),
    )

    mine, kernel_part, input_grad = lax.optimization_barrier((mine, kernel_part, input_grad))
    other = lax.ppermute(mine, "region", swap)
    grads = [((HID, C), F32), ((C, HID), F32)]
    scratch = [((768, C), F32), ((C, 768), F32), ((12,), None)]
    placed = call(
        functools.partial(place_own_kernel, factor),
        grads, scratch, (region, mine), "place_own", 1_000_000, 16, smem=(0,), far=(2, 3),
    )
    vectors = [((HID,), F32)] + [((C,), F32)] * 3
    grad_weight_in, grad_weight_out, grad_bias, grad_gain, grad_shift, grad_scale = call(
        functools.partial(place_other_kernel, factor),
        grads + vectors,
        scratch[:2] + vectors + [((16,), None)],
        (region, other, *placed, mine[0, PART:]), "place_other", 1_000_000, 16,
        smem=(0,), far=(2, 3, 5, 6, 7, 8, 9, 10), aliases={2: 0, 3: 1},
    )
    return (
        output.reshape(features.shape),
        input_grad.reshape(features.shape),
        grad_weight_in,
        grad_weight_out,
        grad_bias,
        grad_gain,
        grad_shift,
        grad_scale,
        kernel_part,
    )


def solution(mesh):
    block = P("chan", "region", None)
    in_specs = (block, block, P(None, "region"), P("chan", None)) + (P(),) * 6
    out_specs = (block, block) + (P(),) * 6 + (P("chan", None),)
    return jax.shard_map(
        per_device, mesh=mesh, in_specs=in_specs, out_specs=out_specs, check_vma=False
    )
```

```python
import functools
import math

import jax
import jax.numpy as jnp
from jax import lax
from jax.experimental import pallas as pl
from jax.experimental.pallas import tpu as pltpu
from jax.sharding import PartitionSpec as P

TS = 16
CH = 24
TILE = 16
PIX = 256
ROWS = CH * TILE
C = 384
HID = 1536
PART = 96
EXTRA = 8
LONG = PART + EXTRA
BRANCH = 32
F32 = jnp.float32
BF = jnp.bfloat16
NT = (((1,), (1,)), ((), ()))
NN = (((1,), (0,)), ((), ()))
TN = (((0,), (0,)), ((), ()))


def iota(shape, dim):
    return lax.broadcasted_iota(jnp.int32, shape, dim)


def dot(left, right, dims=NN):
    return lax.dot_general(left, right, dims, preferred_element_type=F32)


def eye(n):
    return (iota((n, n), 0) == iota((n, n), 1)).astype(F32).astype(BF)


def tile_major():
    column = iota((ROWS, ROWS), 1)
    target = (column & 15) * CH + (column >> 4)
    return (iota((ROWS, ROWS), 0) == target).astype(F32).astype(BF)


def chan_major():
    row = iota((ROWS, ROWS), 0)
    target = (row & 15) * CH + (row >> 4)
    return (iota((ROWS, ROWS), 1) == target).astype(F32).astype(BF)


def one_hots(lookup):
    row = iota((ROWS, 128), 0)
    lane = iota((ROWS, 128), 1)
    key = jnp.where(((row >> 4) & 7) == (lane >> 4), (row >> 7) * 16 + (row & 15), -1)
    parts = [
        (key == lookup[d : d + 1, :]).astype(F32).astype(BF) for d in (0, 4, 5, 1, 6, 7, 2, 3)
    ]
    return jnp.concatenate(parts, axis=1)


def fill_padded(pad, own, low, high, picks):
    for g in range(3):
        lanes = slice(g * 128, (g + 1) * 128)
        table = jnp.concatenate([low[:, lanes], own[:, lanes], high[:, lanes]], axis=1)
        top = dot(table[208:256], picks[:, 0:384])
        bottom = dot(table[0:48], picks[:, 384:768])
        side = dot(table, picks[:, 768:1024])
        pad[g, 3:19, 3:19, :] = own[:, lanes].astype(F32).reshape(16, 16, 128)
        pad[g, 0:3, 3:19, :] = top[:, 0:128].reshape(3, 16, 128)
        pad[g, 0:3, 0:3, :] = top[:, 128:256].reshape(3, 16, 128)[:, 13:16]
        pad[g, 0:3, 19:22, :] = top[:, 256:384].reshape(3, 16, 128)[:, 0:3]
        pad[g, 19:22, 3:19, :] = bottom[:, 0:128].reshape(3, 16, 128)
        pad[g, 19:22, 0:3, :] = bottom[:, 128:256].reshape(3, 16, 128)[:, 13:16]
        pad[g, 19:22, 19:22, :] = bottom[:, 256:384].reshape(3, 16, 128)[:, 0:3]
        pad[g, 3:19, 0:3, :] = side[:, 0:128].reshape(16, 16, 128)[:, 13:16]
        pad[g, 3:19, 19:22, :] = side[:, 128:256].reshape(16, 16, 128)[:, 0:3]


def lookup_rows(region, neighbours, total):
    raw = neighbours[...]
    place = jnp.where(raw >= total, 3 * TILE, raw - (region[0] - 1) * TILE)
    repeat = ((iota((TILE, 128), 1) & 15) == iota((TILE, 128), 0)).astype(F32)
    return dot(place.astype(F32), repeat).astype(jnp.int32)


def spread_taps(kernel, weights):
    member = (iota((CH, ROWS), 0) == (iota((CH, ROWS), 1) >> 4)).astype(F32)
    wide = lax.dot_general(
        kernel, member, TN, preferred_element_type=F32, precision=lax.Precision.HIGHEST
    )
    for g in range(3):
        weights[g] = wide[:, g * 128 : (g + 1) * 128]


def convolve(pad, weights, result, flip):
    def group(g, carry):
        for half in range(2):
            total = [None] * TS
            for b in range(7):
                taps = [
                    weights[g, pl.ds((48 - 7 * a - b) if flip else (7 * a + b), 1), :]
                    for a in range(7)
                ]
                taps = [jnp.broadcast_to(t, (8, 128)) for t in taps]
                for r in range(22):
                    value = pad[g, r, pl.ds(b + 8 * half, 8), :]
                    for a in range(7):
                        i = r - a
                        if 0 <= i < TS:
                            term = taps[a] * value
                            total[i] = term if total[i] is None else total[i] + term
            for i in range(TS):
                result[g, i, pl.ds(8 * half, 8), :] = total[i]
        return carry

    lax.fori_loop(0, 3, group, 0)


def rows_of(result):
    return jnp.concatenate([result[g].reshape(PIX, 128) for g in range(3)], axis=1)


def prepare_kernel(
    total, region, neighbours, own, kernel, cotangent, own_t, upstream, weights, picks, order
):
    spread_taps(kernel[...], weights)
    picks[...] = one_hots(lookup_rows(region, neighbours, total))
    order[...] = tile_major()
    own_t[...] = dot(eye(PIX), own[...], NT).astype(BF)
    upstream[...] = dot(order[...], cotangent[...]).astype(BF)


def sides_of(region, near, far):
    first = region[0] & 1 == 0
    near_t = dot(eye(PIX), near[...], NT)
    far_t = dot(eye(PIX), far[...], NT)
    low = jnp.where(first, far_t, near_t).astype(BF)
    high = jnp.where(first, near_t, far_t).astype(BF)
    return low, high


def forward_kernel(
    region, near, far, own_t, upstream, weights, picks, order, both, pad_out,
    pad, result, conv, sems,
):
    stores = [pltpu.make_async_copy(upstream, both.at[:, pl.ds(PIX, PIX)], sems.at[0])]
    stores[0].start()
    fill_padded(pad, own_t[...], *sides_of(region, near, far), picks)
    pad_out[...] = pad[...].astype(BF)
    convolve(pad, weights, result, False)
    conv[...] = dot(order[...], rows_of(result).astype(BF), NT).astype(BF)
    stores.append(pltpu.make_async_copy(conv, both.at[:, pl.ds(0, PIX)], sems.at[1]))
    stores[1].start()
    for store in stores:
        store.wait()


def taps_kernel(
    received, features, pad_x, output, grad, kernel_grad, unpacked, gradient, sums, pad
):
    for t in range(TILE):
        part = received[t, 0:BRANCH, :].astype(F32)
        rows = slice(t * CH, (t + 1) * CH)
        unpacked[rows, 0:384] = part[0:CH]
        for i in range(3):
            piece = part[CH:, i * 128 : (i + 1) * 128]
            unpacked[t * CH + 8 * i : t * CH + 8 * (i + 1), 384:512] = piece
    both = dot(chan_major(), unpacked[...].astype(BF))
    output[...] = (features[...].astype(F32) + both[:, :PIX]).astype(BF)
    own_grad = both[:, PIX:].astype(BF)
    grad[...] = own_grad
    own = dot(eye(PIX), own_grad, NT)
    for g in range(3):
        gradient[g] = own[:, g * 128 : (g + 1) * 128].reshape(TS, TS, 128)
    sums[...] = jnp.zeros_like(sums)
    pad[...] = pad_x[...].astype(F32)

    def group(g, carry):
        for b in range(7):
            total = [None] * 7
            for half in range(2):
                grads = [gradient[g, i, pl.ds(8 * half, 8), :] for i in range(TS)]
                for r in range(22):
                    value = pad[g, r, pl.ds(b + 8 * half, 8), :]
                    for a in range(7):
                        i = r - a
                        if 0 <= i < TS:
                            term = grads[i] * value
                            total[a] = term if total[a] is None else total[a] + term
            for a in range(7):
                sums[g, pl.ds(7 * a + b, 1), :] = jnp.sum(total[a], axis=0, keepdims=True)
        return carry

    lax.fori_loop(0, 3, group, 0)
    spread = jnp.concatenate([sums[g] for g in range(3)], axis=1)
    member = (iota((32, ROWS), 0) == (iota((32, ROWS), 1) >> 4)).astype(F32)
    total = lax.dot_general(
        member, spread, NT, preferred_element_type=F32, precision=lax.Precision.HIGHEST
    )
    kernel_grad[...] = halves_of(jnp.concatenate([total[8 * i : 8 * i + 8] for i in range(3)], axis=1))


def halves_of(value):
    high = value.astype(BF).astype(F32)
    return jnp.concatenate([high, value - high], axis=1).astype(BF)


def backward_kernel(
    total, region, neighbours, own, near, far, kernel, cotangent, input_grad,
    pad, result, weights, picks,
):
    spread_taps(kernel[...], weights)
    picks[...] = one_hots(lookup_rows(region, neighbours, total))
    own_t = dot(eye(PIX), own[...], NT).astype(BF)
    fill_padded(pad, own_t, *sides_of(region, near, far), picks)
    convolve(pad, weights, result, True)
    upstream = dot(eye(PIX), cotangent[...], NT)
    total = (upstream + rows_of(result)).astype(BF)
    input_grad[...] = dot(eye(ROWS), total, NT).astype(BF)


def normalize(columns):
    values = columns[:, :PIX].astype(F32)
    centered = values - jnp.mean(values, axis=0, keepdims=True)
    inv_std = lax.rsqrt(jnp.mean(centered * centered, axis=0, keepdims=True) + 1e-06)
    return centered * inv_std, inv_std


def stage_kernel(weight_in, weight_out, both):
    both[0:HID, :] = weight_in[...]
    for q in range(4):
        both[HID + q * C : HID + (q + 1) * C, :] = weight_out[:, q * C : (q + 1) * C]


def hidden_blocks(
    side, table, inputs, grad_mixed, bias, matrices, parts, mixed_out, grad_inputs, small,
):
    lane = iota((C, 128), 1)
    for q in range(4):
        bias[q * C : (q + 1) * C, :] = table[:, q : q + 1]
    for k in range(2):
        block = 2 * side + k
        rows = pl.ds(pl.multiple_of(block * C, C), C)
        weight_in = matrices[rows, :]
        weight_out = matrices[pl.ds(pl.multiple_of(HID + block * C, C), C), :]
        hidden = dot(weight_in, inputs) + bias[rows, :]
        cdf = 0.5 + 0.5 * lax.erf(hidden * 0.7071067811865476)
        activation = (hidden * cdf).astype(BF)
        slope = cdf + hidden * jnp.exp(-0.5 * hidden * hidden) * 0.3989422804014327
        mixed_out = mixed_out + dot(weight_out, activation)
        grad_hidden = dot(weight_out, grad_mixed, TN) * slope
        small = small + jnp.where(
            lane == block, jnp.sum(grad_hidden, axis=1, keepdims=True), 0.0
        )
        hidden_grad = grad_hidden.astype(BF)
        grad_inputs = grad_inputs + dot(weight_in, hidden_grad, TN)
        part = dot(hidden_grad, inputs, NT).astype(BF)
        for s in range(4):
            parts[4 * k + s] = part[s * PART : (s + 1) * PART]
        part = dot(grad_mixed, activation, NT).astype(BF)
        for s in range(4):
            parts[8 + 4 * k + s] = part[s * PART : (s + 1) * PART]
    return mixed_out, grad_inputs, small


def first_half_kernel(
    region, columns, vectors, matrices,
    parts, mixed_sum, grad_sum, small_sum, bias,
):
    table = jnp.transpose(vectors[...])
    normed, _ = normalize(columns)
    inputs = (normed * table[:, 4:5] + table[:, 5:6]).astype(BF)
    grad_mixed = (table[:, 6:7] * columns[:, PIX:].astype(F32)).astype(BF)
    zeros = jnp.zeros((C, PIX), F32)
    mixed_sum[...], grad_sum[...], small_sum[...] = hidden_blocks(
        1 - (region[0] & 1), table, inputs, grad_mixed, bias,
        matrices, parts, zeros, zeros, jnp.zeros((C, 128), F32),
    )


def second_half_kernel(
    region, columns, vectors, matrices,
    mixed_sum, grad_sum, small_sum, out, parts, extra, bias,
):
    table = jnp.transpose(vectors[...])
    gain = table[:, 4:5]
    scale = table[:, 6:7]
    normed, inv_std = normalize(columns)
    inputs = (normed * gain + table[:, 5:6]).astype(BF)
    upstream = columns[:, PIX:].astype(F32)
    grad_mixed = (scale * upstream).astype(BF)
    mixed_out, grad_inputs, small = hidden_blocks(
        region[0] & 1, table, inputs, grad_mixed, bias,
        matrices, parts, mixed_sum[...], grad_sum[...], small_sum[...],
    )
    branch = scale * mixed_out
    grad_scale = jnp.sum(upstream * mixed_out, axis=1, keepdims=True)
    grad_gain = jnp.sum(grad_inputs * normed, axis=1, keepdims=True)
    grad_shift = jnp.sum(grad_inputs, axis=1, keepdims=True)
    grad_normed = grad_inputs * gain
    grad_conv = (
        grad_normed
        - jnp.mean(grad_normed, axis=0, keepdims=True)
        - normed * jnp.mean(grad_normed * normed, axis=0, keepdims=True)
    ) * inv_std
    for j in range(16):
        rows = slice(j * CH, (j + 1) * CH)
        side = grad_conv[rows, 128:]
        first = jnp.concatenate([branch[rows], grad_conv[rows, :128]], axis=1)
        last = jnp.concatenate([side[8 * i : 8 * i + 8] for i in range(3)], axis=1)
        out[j] = jnp.concatenate([first, last], axis=0).astype(BF)
    lane = iota((C, 128), 1)
    small = small + jnp.where(lane == 4, grad_gain, 0.0)
    small = small + jnp.where(lane == 5, grad_shift, 0.0)
    small = small + jnp.where(lane == 6, grad_scale, 0.0)
    extra[...] = jnp.transpose(small)[0:EXTRA].astype(BF)


def add_kernel(out, first, second, total):
    total[:, 0:BRANCH, :] = out[...]
    total[:, BRANCH:, :] = (first[...].astype(F32) + second[...].astype(F32)).astype(BF)


def first_step_kernel(sent, got, kernel_grad, total):
    total[0:LONG, :] = (sent[...].astype(F32) + got[...].astype(F32)).astype(BF)
    total[LONG:, :] = kernel_grad[...]


def joined(sent, got):
    value = sent[...].astype(F32) + got[...].astype(F32)
    return value[0:LONG].astype(BF), value[LONG:, :192] + value[LONG:, 192:]


def next_step_kernel(sent, got, total):
    weights, taps = joined(sent, got)
    total[0:LONG, :] = weights
    total[LONG:, :] = halves_of(taps)


def spread_kernel(sent, got, total, kernel_grad, value, sems):
    value[...], kernel_grad[...] = joined(sent, got)
    stores = [pltpu.make_async_copy(value, total.at[j], sems.at[j]) for j in range(16)]
    for store in stores:
        store.start()
    for store in stores:
        store.wait()


def place(factor, side, ref, grad_in, grad_out, tall, wide, sems):
    half = pl.multiple_of(side * 768, 768)
    stores = []
    for j in range(8):
        rows = pl.ds(j * PART, PART)
        tall[rows, :] = ref[j, 0:PART, :].astype(F32) * factor
        target = grad_in.at[pl.ds(half + j * PART, PART), :]
        stores.append(pltpu.make_async_copy(tall.at[rows, :], target, sems.at[j]))
        stores[-1].start()
    for s in range(4):
        rows = pl.ds(s * PART, PART)
        for k in range(2):
            wide[rows, k * C : (k + 1) * C] = ref[8 + 4 * k + s, 0:PART, :].astype(F32) * factor
        target = grad_out.at[rows, pl.ds(half, 768)]
        stores.append(pltpu.make_async_copy(wide.at[rows, :], target, sems.at[8 + s]))
        stores[-1].start()
    return stores


def place_own_kernel(factor, region, ref, grad_in, grad_out, tall, wide, sems):
    for store in place(factor, region[0] & 1, ref, grad_in, grad_out, tall, wide, sems):
        store.wait()


def place_other_kernel(
    factor, region, ref, in_a, out_a, own_extra, grad_in, grad_out, bias, gain, shift, scale,
    tall, wide, bias_ref, gain_ref, shift_ref, scale_ref, sems,
):
    stores = place(factor, 1 - (region[0] & 1), ref, grad_in, grad_out, tall, wide, sems)
    small = ref[0, PART:, :].astype(F32)
    for j in range(1, 16):
        small = small + ref[j, PART:, :].astype(F32)
    small = (own_extra[...] + small) * factor
    for q in range(4):
        bias_ref[q * C : (q + 1) * C] = small[q]
    gain_ref[...] = small[4]
    shift_ref[...] = small[5]
    scale_ref[...] = small[6]
    pairs = [(bias_ref, bias), (gain_ref, gain), (shift_ref, shift), (scale_ref, scale)]
    for i, pair in enumerate(pairs):
        stores.append(pltpu.make_async_copy(*pair, sems.at[12 + i]))
        stores[-1].start()
    for store in stores:
        store.wait()


def call(
    body, shapes, scratch, args, name, flops, limit, smem=(), far=(), anywhere=(), aliases=None
):
    spaces = [pltpu.VMEM] * (len(args) + len(shapes))
    for space, places in ((pltpu.SMEM, smem), (pltpu.HBM, far), (pl.ANY, anywhere)):
        for i in places:
            spaces[i] = space
    spaces = [pl.BlockSpec(memory_space=space) for space in spaces]
    moved = sum(a.size * a.dtype.itemsize for a in args)
    moved += sum(math.prod(s) * jnp.dtype(d).itemsize for s, d in shapes)
    return pl.pallas_call(
        body,
        out_shape=[jax.ShapeDtypeStruct(s, d) for s, d in shapes],
        in_specs=spaces[: len(args)],
        out_specs=spaces[len(args) :],
        scratch_shapes=[
            pltpu.SemaphoreType.DMA(s) if d is None else pltpu.VMEM(s, d) for s, d in scratch
        ],
        compiler_params=pltpu.CompilerParams(vmem_limit_bytes=int(limit * 1024 * 1024)),
        cost_estimate=pl.CostEstimate(flops=flops, bytes_accessed=moved, transcendentals=0),
        input_output_aliases=aliases or {},
        name=name,
    )(*args)


def both_sides(field):
    count = lax.axis_size("region")
    near = [(i, i ^ 1) for i in range(count)]
    far = [(i, ((i + 1) ^ 1) - 1) for i in range(1, count - 1)]
    return lax.ppermute(field, "region", near), lax.ppermute(field, "region", far)


def cube_pairs(count, bit, core=0):
    ring = count // 2
    label = [z ^ (z >> 1) for z in range(ring)]
    place = {g: z for z, g in enumerate(label)}
    return [
        (2 * z + c, 2 * place[label[z] ^ bit] + (c ^ core)) for z in range(ring) for c in range(2)
    ]


def sum_four(value, first, second, both):
    near, far, across = (lax.ppermute(value, "region", pairs) for pairs in (first, second, both))
    return (value + near) + (far + across)


def per_device(
    features, cotangent, neighbours, kernel, norm_gain, norm_shift,
    weight_in, bias_in, weight_out, layer_scale,
):
    count = lax.axis_size("region")
    peers = lax.axis_size("chan")
    region = lax.axis_index("region").astype(jnp.int32).reshape(1)
    total_tiles = TILE * count
    factor = 1.0 / math.sqrt(total_tiles * PIX)
    swap = [(i, i ^ 1) for i in range(count)]

    x = features.reshape(ROWS, PIX)
    upstream = cotangent.reshape(ROWS, PIX)
    x_near, x_far = both_sides(x)
    vectors = jnp.concatenate(
        [
            bias_in.reshape(4, C), norm_gain[None], norm_shift[None], layer_scale[None],
            jnp.zeros((1, C), F32),
        ],
        axis=0,
    )

    padded = ((3, 22, 24, 128), F32)
    square = ((3, 16, 16, 128), F32)
    taps = ((3, 49, 128), F32)
    block = ((ROWS, PIX), BF)
    ready = call(
        functools.partial(prepare_kernel, total_tiles),
        [((PIX, ROWS), BF), block, taps, ((ROWS, 1024), BF), ((ROWS, ROWS), BF)],
        [],
        (region, neighbours, x, kernel, upstream),
        "prepare",
        200_000_000,
        16,
        smem=(0,),
    )
    columns, pad_x = call(
        forward_kernel,
        [((ROWS, 2 * PIX), BF), (padded[0], BF)],
        [padded, square, block, ((2,), None)],
        (region, x_near, x_far, *ready),
        "forward_conv",
        400_000_000,
        16,
        smem=(0,),
        far=(8,),
    )
    columns = lax.all_to_all(columns, "chan", split_axis=0, concat_axis=0, tiled=True)

    staged = call(
        stage_kernel, [((2 * HID, C), BF)], [], (weight_in, weight_out),
        "stage", 1_000_000, 8,
    )
    halves = (16, PART, C)
    pixels = (region, columns, vectors, *staged)
    scratch = [((HID, 1), F32)]
    sums = [((C, PIX), F32), ((C, PIX), F32), ((C, 128), F32)]
    send, *partial = call(
        first_half_kernel,
        [(halves, BF)] + sums,
        scratch,
        pixels,
        "pixels_first",
        1_000_000_000,
        24,
        smem=(0,),
    )
    partner = lax.ppermute(send, "region", swap)
    out, keep, extra = call(
        second_half_kernel,
        [((16, BRANCH, C), BF), (halves, BF), ((EXTRA, C), BF)],
        scratch,
        (*pixels, *partial),
        "pixels_second",
        1_000_000_000,
        24,
        smem=(0,),
    )
    (travel,) = call(
        add_kernel, [((16, BRANCH + PART, C), BF)], [], (out, keep, partner), "add_cores", 1_000_000, 8
    )
    travel = lax.all_to_all(travel, "chan", split_axis=0, concat_axis=0, tiled=True)

    sent = jnp.sum(travel[:, BRANCH:].astype(F32), axis=0).astype(BF)
    sent = jnp.concatenate([sent, extra], axis=0)
    got = lax.ppermute(sent, "region", cube_pairs(count, 1))
    output, grad, kernel_part = call(
        taps_kernel,
        [((ROWS, PIX), BF), ((ROWS, PIX), BF), ((8, C), BF)],
        [((ROWS, 2 * PIX), F32), square, ((3, 64, 128), F32), padded],
        (travel, x, pad_x),
        "kernel_taps",
        400_000_000,
        16,
    )
    step = [((LONG + 8, C), BF)]
    (sent,) = call(first_step_kernel, step, [], (sent, got, kernel_part), "step", 100_000, 4)
    got = lax.ppermute(sent, "region", cube_pairs(count, 2))
    (sent,) = call(next_step_kernel, step, [], (sent, got), "step", 100_000, 4)
    got = lax.ppermute(sent, "region", cube_pairs(count, 4))
    mine, kernel_part = call(
        spread_kernel, [((peers, LONG, C), BF), ((8, 192), F32)],
        [((LONG, C), BF), ((16,), None)], (sent, got), "spread", 1_000_000, 8, far=(2,),
    )
    mine = lax.all_to_all(mine, "chan", split_axis=0, concat_axis=0, tiled=True)

    grad_near, grad_far = both_sides(grad)
    kernel_part = sum_four(kernel_part, swap, cube_pairs(count, 1), cube_pairs(count, 1, 1))
    (input_grad,) = call(
        functools.partial(backward_kernel, total_tiles),
        [block],
        [padded, square, taps, ((ROWS, 1024), BF)],
        (region, neighbours, grad, grad_near, grad_far, kernel, upstream),
        "backward_conv",
        400_000_000,
        16,
        smem=(0,),
    )

    mine, kernel_part, input_grad = lax.optimization_barrier((mine, kernel_part, input_grad))
    other = lax.ppermute(mine, "region", swap)
    kernel_part = kernel_part.reshape(8, 3, 64).transpose(1, 0, 2).reshape(CH, 64)
    kernel_part = kernel_part[:, :49] * factor
    grads = [((HID, C), F32), ((C, HID), F32)]
    scratch = [((768, C), F32), ((C, 768), F32), ((12,), None)]
    placed = call(
        functools.partial(place_own_kernel, factor),
        grads, scratch, (region, mine), "place_own", 1_000_000, 16, smem=(0,), far=(2, 3),
    )
    own_extra = mine[0, PART:].astype(F32)
    for j in range(1, peers):
        own_extra = own_extra + mine[j, PART:].astype(F32)
    vectors = [((HID,), F32)] + [((C,), F32)] * 3
    grad_weight_in, grad_weight_out, grad_bias, grad_gain, grad_shift, grad_scale = call(
        functools.partial(place_other_kernel, factor),
        grads + vectors,
        scratch[:2] + vectors + [((16,), None)],
        (region, other, *placed, own_extra), "place_other", 1_000_000, 16,
        smem=(0,), far=(2, 3, 5, 6, 7, 8, 9, 10), aliases={2: 0, 3: 1},
    )
    return (
        output.reshape(features.shape),
        input_grad.reshape(features.shape),
        grad_weight_in,
        grad_weight_out,
        grad_bias,
        grad_gain,
        grad_shift,
        grad_scale,
        kernel_part,
    )


def solution(mesh):
    block = P("chan", "region", None)
    in_specs = (block, block, P(None, "region"), P("chan", None)) + (P(),) * 6
    out_specs = (block, block) + (P(),) * 6 + (P("chan", None),)
    return jax.shard_map(
        per_device, mesh=mesh, in_specs=in_specs, out_specs=out_specs, check_vma=False
    )
```

```python
import functools
import math

import jax
import jax.numpy as jnp
from jax import lax
from jax.experimental import pallas as pl
from jax.experimental.pallas import tpu as pltpu
from jax.sharding import PartitionSpec as P

TS = 16
CH = 24
TILE = 16
PIX = 256
ROWS = CH * TILE
C = 384
HID = 1536
PART = 96
EXTRA = 8
LONG = PART + EXTRA
BRANCH = 32
F32 = jnp.float32
BF = jnp.bfloat16
NT = (((1,), (1,)), ((), ()))
NN = (((1,), (0,)), ((), ()))
TN = (((0,), (0,)), ((), ()))


def iota(shape, dim):
    return lax.broadcasted_iota(jnp.int32, shape, dim)


def dot(left, right, dims=NN):
    return lax.dot_general(left, right, dims, preferred_element_type=F32)


def eye(n):
    return (iota((n, n), 0) == iota((n, n), 1)).astype(F32).astype(BF)


def tile_major():
    column = iota((ROWS, ROWS), 1)
    target = (column & 15) * CH + (column >> 4)
    return (iota((ROWS, ROWS), 0) == target).astype(F32).astype(BF)


def chan_major():
    row = iota((ROWS, ROWS), 0)
    target = (row & 15) * CH + (row >> 4)
    return (iota((ROWS, ROWS), 1) == target).astype(F32).astype(BF)


def one_hots(lookup):
    row = iota((ROWS, 128), 0)
    lane = iota((ROWS, 128), 1)
    key = jnp.where(((row >> 4) & 7) == (lane >> 4), (row >> 7) * 16 + (row & 15), -1)
    parts = [
        (key == lookup[d : d + 1, :]).astype(F32).astype(BF) for d in (0, 4, 5, 1, 6, 7, 2, 3)
    ]
    return jnp.concatenate(parts, axis=1)


def fill_padded(pad, own, low, high, picks):
    apart = jnp.concatenate([picks[0:128, :], picks[256:384, :]], axis=0)
    for g in range(3):
        lanes = slice(g * 128, (g + 1) * 128)
        mine = own[:, lanes]
        sides = jnp.concatenate([low[lanes, :], high[lanes, :]], axis=0)

        def take(span, first, last):
            spread = dot(sides[:, span], apart[:, first:last], TN)
            return spread + dot(mine[span], picks[128:256, first:last])

        top = take(slice(128, 256), 0, 384)[80:128]
        bottom = take(slice(0, 128), 384, 768)[0:48]
        side = take(slice(0, 256), 768, 1024)
        pad[g, 3:19, 3:19, :] = own[:, lanes].astype(F32).reshape(16, 16, 128)
        pad[g, 0:3, 3:19, :] = top[:, 0:128].reshape(3, 16, 128)
        pad[g, 0:3, 0:3, :] = top[:, 128:256].reshape(3, 16, 128)[:, 13:16]
        pad[g, 0:3, 19:22, :] = top[:, 256:384].reshape(3, 16, 128)[:, 0:3]
        pad[g, 19:22, 3:19, :] = bottom[:, 0:128].reshape(3, 16, 128)
        pad[g, 19:22, 0:3, :] = bottom[:, 128:256].reshape(3, 16, 128)[:, 13:16]
        pad[g, 19:22, 19:22, :] = bottom[:, 256:384].reshape(3, 16, 128)[:, 0:3]
        pad[g, 3:19, 0:3, :] = side[:, 0:128].reshape(16, 16, 128)[:, 13:16]
        pad[g, 3:19, 19:22, :] = side[:, 128:256].reshape(16, 16, 128)[:, 0:3]


def lookup_rows(region, neighbours, total):
    raw = neighbours[...]
    place = jnp.where(raw >= total, 3 * TILE, raw - (region[0] - 1) * TILE)
    repeat = ((iota((TILE, 128), 1) & 15) == iota((TILE, 128), 0)).astype(F32)
    return dot(place.astype(F32), repeat).astype(jnp.int32)


def spread_taps(kernel, weights):
    member = (iota((CH, ROWS), 0) == (iota((CH, ROWS), 1) >> 4)).astype(F32)
    wide = lax.dot_general(
        kernel, member, TN, preferred_element_type=F32, precision=lax.Precision.HIGHEST
    )
    for g in range(3):
        weights[g] = wide[:, g * 128 : (g + 1) * 128]


def convolve(pad, weights, result, flip):
    def group(g):
        for half in range(2):
            total = [None] * TS
            for b in range(7):
                taps = [
                    weights[g, pl.ds((48 - 7 * a - b) if flip else (7 * a + b), 1), :]
                    for a in range(7)
                ]
                taps = [jnp.broadcast_to(t, (8, 128)) for t in taps]
                for r in range(22):
                    value = pad[g, r, pl.ds(b + 8 * half, 8), :]
                    for a in range(7):
                        i = r - a
                        if 0 <= i < TS:
                            term = taps[a] * value
                            total[i] = term if total[i] is None else total[i] + term
            for i in range(TS):
                result[g, i, pl.ds(8 * half, 8), :] = total[i]

    for g in range(3):
        group(g)


def rows_of(result):
    return jnp.concatenate([result[g].reshape(PIX, 128) for g in range(3)], axis=1)


def prepare_kernel(
    total, region, neighbours, own, kernel, cotangent, own_t, upstream, weights, picks, order
):
    spread_taps(kernel[...], weights)
    picks[...] = one_hots(lookup_rows(region, neighbours, total))
    order[...] = tile_major()
    own_t[...] = dot(eye(PIX), own[...], NT).astype(BF)
    upstream[...] = dot(order[...], cotangent[...]).astype(BF)


def sides_of(region, near, far):
    first = region[0] & 1 == 0
    low = jnp.where(first, far[...], near[...])
    high = jnp.where(first, near[...], far[...])
    return low, high


def forward_kernel(
    region, near, far, own_t, upstream, weights, picks, order, both, pad_out,
    pad, result, conv, sems,
):
    stores = [pltpu.make_async_copy(upstream, both.at[:, pl.ds(PIX, PIX)], sems.at[0])]
    stores[0].start()
    fill_padded(pad, own_t[...], *sides_of(region, near, far), picks)
    pad_out[...] = pad[...].astype(BF)
    convolve(pad, weights, result, False)
    conv[...] = dot(order[...], rows_of(result).astype(BF), NT).astype(BF)
    stores.append(pltpu.make_async_copy(conv, both.at[:, pl.ds(0, PIX)], sems.at[1]))
    stores[1].start()
    for store in stores:
        store.wait()


def taps_kernel(
    received, features, pad_x, output, grad, kernel_grad, unpacked, gradient, sums, pad
):
    for t in range(TILE):
        part = received[t, 0:BRANCH, :].astype(F32)
        rows = slice(t * CH, (t + 1) * CH)
        unpacked[rows, 0:384] = part[0:CH]
        for i in range(3):
            piece = part[CH:, i * 128 : (i + 1) * 128]
            unpacked[t * CH + 8 * i : t * CH + 8 * (i + 1), 384:512] = piece
    both = dot(chan_major(), unpacked[...].astype(BF))
    output[...] = (features[...].astype(F32) + both[:, :PIX]).astype(BF)
    own_grad = both[:, PIX:].astype(BF)
    grad[...] = own_grad
    own = dot(eye(PIX), own_grad, NT)
    for g in range(3):
        gradient[g] = own[:, g * 128 : (g + 1) * 128].reshape(TS, TS, 128)
    sums[...] = jnp.zeros_like(sums)
    pad[...] = pad_x[...].astype(F32)

    def group(g):
        for b in range(7):
            total = [None] * 7
            for half in range(2):
                grads = [gradient[g, i, pl.ds(8 * half, 8), :] for i in range(TS)]
                for r in range(22):
                    value = pad[g, r, pl.ds(b + 8 * half, 8), :]
                    for a in range(7):
                        i = r - a
                        if 0 <= i < TS:
                            term = grads[i] * value
                            total[a] = term if total[a] is None else total[a] + term
            for a in range(7):
                sums[g, pl.ds(7 * a + b, 1), :] = jnp.sum(total[a], axis=0, keepdims=True)

    for g in range(3):
        group(g)
    spread = jnp.concatenate([sums[g] for g in range(3)], axis=1)
    member = (iota((32, ROWS), 0) == (iota((32, ROWS), 1) >> 4)).astype(F32)
    total = lax.dot_general(
        member, spread, NT, preferred_element_type=F32, precision=lax.Precision.HIGHEST
    )
    kernel_grad[...] = halves_of(jnp.concatenate([total[8 * i : 8 * i + 8] for i in range(3)], axis=1))


def halves_of(value):
    high = value.astype(BF).astype(F32)
    return jnp.concatenate([high, value - high], axis=1).astype(BF)


def backward_kernel(
    total, region, neighbours, own, near, far, kernel, cotangent, input_grad,
    pad, result, weights, picks,
):
    spread_taps(kernel[...], weights)
    picks[...] = one_hots(lookup_rows(region, neighbours, total))
    own_t = dot(eye(PIX), own[...], NT).astype(BF)
    fill_padded(pad, own_t, *sides_of(region, near, far), picks)
    convolve(pad, weights, result, True)
    upstream = dot(eye(PIX), cotangent[...], NT)
    total = (upstream + rows_of(result)).astype(BF)
    input_grad[...] = dot(eye(ROWS), total, NT).astype(BF)


def normalize(columns):
    values = columns[:, :PIX].astype(F32)
    centered = values - jnp.mean(values, axis=0, keepdims=True)
    inv_std = lax.rsqrt(jnp.mean(centered * centered, axis=0, keepdims=True) + 1e-06)
    return centered * inv_std, inv_std


def stage_kernel(weight_in, weight_out, both):
    both[0:HID, :] = weight_in[...]
    for q in range(4):
        both[HID + q * C : HID + (q + 1) * C, :] = weight_out[:, q * C : (q + 1) * C]


def hidden_blocks(
    side, table, inputs, grad_mixed, bias, matrices, parts, mixed_out, grad_inputs, small,
):
    lane = iota((C, 128), 1)
    for q in range(4):
        bias[q * C : (q + 1) * C, :] = table[:, q : q + 1]
    for k in range(2):
        block = 2 * side + k
        rows = pl.ds(pl.multiple_of(block * C, C), C)
        weight_in = matrices[rows, :]
        weight_out = matrices[pl.ds(pl.multiple_of(HID + block * C, C), C), :]
        hidden = dot(weight_in, inputs) + bias[rows, :]
        cdf = 0.5 + 0.5 * lax.erf(hidden * 0.7071067811865476)
        activation = (hidden * cdf).astype(BF)
        slope = cdf + hidden * jnp.exp(-0.5 * hidden * hidden) * 0.3989422804014327
        mixed_out = mixed_out + dot(weight_out, activation)
        grad_hidden = dot(weight_out, grad_mixed, TN) * slope
        small = small + jnp.where(
            lane == block, jnp.sum(grad_hidden, axis=1, keepdims=True), 0.0
        )
        hidden_grad = grad_hidden.astype(BF)
        grad_inputs = grad_inputs + dot(weight_in, hidden_grad, TN)
        part = dot(hidden_grad, inputs, NT).astype(BF)
        for s in range(4):
            parts[4 * k + s] = part[s * PART : (s + 1) * PART]
        part = dot(grad_mixed, activation, NT).astype(BF)
        for s in range(4):
            parts[8 + 4 * k + s] = part[s * PART : (s + 1) * PART]
    return mixed_out, grad_inputs, small


def first_half_kernel(
    region, columns, vectors, matrices,
    parts, mixed_sum, grad_sum, small_sum, bias,
):
    table = jnp.transpose(vectors[...])
    normed, _ = normalize(columns)
    inputs = (normed * table[:, 4:5] + table[:, 5:6]).astype(BF)
    grad_mixed = (table[:, 6:7] * columns[:, PIX:].astype(F32)).astype(BF)
    zeros = jnp.zeros((C, PIX), F32)
    mixed_sum[...], grad_sum[...], small_sum[...] = hidden_blocks(
        1 - (region[0] & 1), table, inputs, grad_mixed, bias,
        matrices, parts, zeros, zeros, jnp.zeros((C, 128), F32),
    )


def second_half_kernel(
    region, columns, vectors, matrices,
    mixed_sum, grad_sum, small_sum, out, parts, extra, bias,
):
    table = jnp.transpose(vectors[...])
    gain = table[:, 4:5]
    scale = table[:, 6:7]
    normed, inv_std = normalize(columns)
    inputs = (normed * gain + table[:, 5:6]).astype(BF)
    upstream = columns[:, PIX:].astype(F32)
    grad_mixed = (scale * upstream).astype(BF)
    mixed_out, grad_inputs, small = hidden_blocks(
        region[0] & 1, table, inputs, grad_mixed, bias,
        matrices, parts, mixed_sum[...], grad_sum[...], small_sum[...],
    )
    branch = scale * mixed_out
    grad_scale = jnp.sum(upstream * mixed_out, axis=1, keepdims=True)
    grad_gain = jnp.sum(grad_inputs * normed, axis=1, keepdims=True)
    grad_shift = jnp.sum(grad_inputs, axis=1, keepdims=True)
    grad_normed = grad_inputs * gain
    grad_conv = (
        grad_normed
        - jnp.mean(grad_normed, axis=0, keepdims=True)
        - normed * jnp.mean(grad_normed * normed, axis=0, keepdims=True)
    ) * inv_std
    for j in range(16):
        rows = slice(j * CH, (j + 1) * CH)
        side = grad_conv[rows, 128:]
        first = jnp.concatenate([branch[rows], grad_conv[rows, :128]], axis=1)
        last = jnp.concatenate([side[8 * i : 8 * i + 8] for i in range(3)], axis=1)
        out[j] = jnp.concatenate([first, last], axis=0).astype(BF)
    lane = iota((C, 128), 1)
    small = small + jnp.where(lane == 4, grad_gain, 0.0)
    small = small + jnp.where(lane == 5, grad_shift, 0.0)
    small = small + jnp.where(lane == 6, grad_scale, 0.0)
    extra[...] = jnp.transpose(small)[0:EXTRA].astype(BF)


def add_kernel(out, first, second, total):
    total[:, 0:BRANCH, :] = out[...]
    total[:, BRANCH:, :] = (first[...].astype(F32) + second[...].astype(F32)).astype(BF)


def first_step_kernel(sent, got, kernel_grad, total):
    total[0:LONG, :] = (sent[...].astype(F32) + got[...].astype(F32)).astype(BF)
    total[LONG:, :] = kernel_grad[...]


def joined(sent, got):
    value = sent[...].astype(F32) + got[...].astype(F32)
    return value[0:LONG].astype(BF), value[LONG:, :192] + value[LONG:, 192:]


def next_step_kernel(sent, got, total):
    weights, taps = joined(sent, got)
    total[0:LONG, :] = weights
    total[LONG:, :] = halves_of(taps)


def spread_kernel(sent, got, total, kernel_grad, value, sems):
    value[...], kernel_grad[...] = joined(sent, got)
    stores = [pltpu.make_async_copy(value, total.at[j], sems.at[j]) for j in range(16)]
    for store in stores:
        store.start()
    for store in stores:
        store.wait()


def place(factor, side, ref, grad_in, grad_out, tall, wide, sems):
    half = pl.multiple_of(side * 768, 768)
    stores = []
    for j in range(8):
        rows = pl.ds(j * PART, PART)
        tall[rows, :] = ref[j, 0:PART, :].astype(F32) * factor
        target = grad_in.at[pl.ds(half + j * PART, PART), :]
        stores.append(pltpu.make_async_copy(tall.at[rows, :], target, sems.at[j]))
        stores[-1].start()
    for s in range(4):
        rows = pl.ds(s * PART, PART)
        for k in range(2):
            wide[rows, k * C : (k + 1) * C] = ref[8 + 4 * k + s, 0:PART, :].astype(F32) * factor
        target = grad_out.at[rows, pl.ds(half, 768)]
        stores.append(pltpu.make_async_copy(wide.at[rows, :], target, sems.at[8 + s]))
        stores[-1].start()
    return stores


def place_own_kernel(factor, region, ref, grad_in, grad_out, tall, wide, sems):
    for store in place(factor, region[0] & 1, ref, grad_in, grad_out, tall, wide, sems):
        store.wait()


def place_other_kernel(
    factor, region, ref, in_a, out_a, own_extra, grad_in, grad_out, bias, gain, shift, scale,
    tall, wide, bias_ref, gain_ref, shift_ref, scale_ref, sems,
):
    stores = place(factor, 1 - (region[0] & 1), ref, grad_in, grad_out, tall, wide, sems)
    small = ref[0, PART:, :].astype(F32)
    for j in range(1, 16):
        small = small + ref[j, PART:, :].astype(F32)
    small = (own_extra[...] + small) * factor
    for q in range(4):
        bias_ref[q * C : (q + 1) * C] = small[q]
    gain_ref[...] = small[4]
    shift_ref[...] = small[5]
    scale_ref[...] = small[6]
    pairs = [(bias_ref, bias), (gain_ref, gain), (shift_ref, shift), (scale_ref, scale)]
    for i, pair in enumerate(pairs):
        stores.append(pltpu.make_async_copy(*pair, sems.at[12 + i]))
        stores[-1].start()
    for store in stores:
        store.wait()


def call(
    body, shapes, scratch, args, name, flops, limit, smem=(), far=(), anywhere=(), aliases=None
):
    spaces = [pltpu.VMEM] * (len(args) + len(shapes))
    for space, places in ((pltpu.SMEM, smem), (pltpu.HBM, far), (pl.ANY, anywhere)):
        for i in places:
            spaces[i] = space
    spaces = [pl.BlockSpec(memory_space=space) for space in spaces]
    moved = sum(a.size * a.dtype.itemsize for a in args)
    moved += sum(math.prod(s) * jnp.dtype(d).itemsize for s, d in shapes)
    return pl.pallas_call(
        body,
        out_shape=[jax.ShapeDtypeStruct(s, d) for s, d in shapes],
        in_specs=spaces[: len(args)],
        out_specs=spaces[len(args) :],
        scratch_shapes=[
            pltpu.SemaphoreType.DMA(s) if d is None else pltpu.VMEM(s, d) for s, d in scratch
        ],
        compiler_params=pltpu.CompilerParams(vmem_limit_bytes=int(limit * 1024 * 1024)),
        cost_estimate=pl.CostEstimate(flops=flops, bytes_accessed=moved, transcendentals=0),
        input_output_aliases=aliases or {},
        name=name,
    )(*args)


def both_sides(field):
    count = lax.axis_size("region")
    near = [(i, i ^ 1) for i in range(count)]
    far = [(i, ((i + 1) ^ 1) - 1) for i in range(1, count - 1)]
    return lax.ppermute(field, "region", near), lax.ppermute(field, "region", far)


def cube_pairs(count, bit, core=0):
    ring = count // 2
    label = [z ^ (z >> 1) for z in range(ring)]
    place = {g: z for z, g in enumerate(label)}
    return [
        (2 * z + c, 2 * place[label[z] ^ bit] + (c ^ core)) for z in range(ring) for c in range(2)
    ]


def sum_four(value, first, second, both):
    near, far, across = (lax.ppermute(value, "region", pairs) for pairs in (first, second, both))
    return (value + near) + (far + across)


def per_device(
    features, cotangent, neighbours, kernel, norm_gain, norm_shift,
    weight_in, bias_in, weight_out, layer_scale,
):
    count = lax.axis_size("region")
    peers = lax.axis_size("chan")
    region = lax.axis_index("region").astype(jnp.int32).reshape(1)
    total_tiles = TILE * count
    factor = 1.0 / math.sqrt(total_tiles * PIX)
    swap = [(i, i ^ 1) for i in range(count)]

    x = features.reshape(ROWS, PIX)
    upstream = cotangent.reshape(ROWS, PIX)
    x_near, x_far = both_sides(x)
    vectors = jnp.concatenate(
        [
            bias_in.reshape(4, C), norm_gain[None], norm_shift[None], layer_scale[None],
            jnp.zeros((1, C), F32),
        ],
        axis=0,
    )

    padded = ((3, 22, 24, 128), F32)
    square = ((3, 16, 16, 128), F32)
    taps = ((3, 49, 128), F32)
    block = ((ROWS, PIX), BF)
    ready = call(
        functools.partial(prepare_kernel, total_tiles),
        [((PIX, ROWS), BF), block, taps, ((ROWS, 1024), BF), ((ROWS, ROWS), BF)],
        [],
        (region, neighbours, x, kernel, upstream),
        "prepare",
        200_000_000,
        16,
        smem=(0,),
    )
    columns, pad_x = call(
        forward_kernel,
        [((ROWS, 2 * PIX), BF), (padded[0], BF)],
        [padded, square, block, ((2,), None)],
        (region, x_near, x_far, *ready),
        "forward_conv",
        400_000_000,
        16,
        smem=(0,),
        far=(8,),
    )
    columns = lax.all_to_all(columns, "chan", split_axis=0, concat_axis=0, tiled=True)

    staged = call(
        stage_kernel, [((2 * HID, C), BF)], [], (weight_in, weight_out),
        "stage", 1_000_000, 8,
    )
    halves = (16, PART, C)
    pixels = (region, columns, vectors, *staged)
    scratch = [((HID, 1), F32)]
    sums = [((C, PIX), F32), ((C, PIX), F32), ((C, 128), F32)]
    send, *partial = call(
        first_half_kernel,
        [(halves, BF)] + sums,
        scratch,
        pixels,
        "pixels_first",
        1_000_000_000,
        24,
        smem=(0,),
    )
    partner = lax.ppermute(send, "region", swap)
    out, keep, extra = call(
        second_half_kernel,
        [((16, BRANCH, C), BF), (halves, BF), ((EXTRA, C), BF)],
        scratch,
        (*pixels, *partial),
        "pixels_second",
        1_000_000_000,
        24,
        smem=(0,),
    )
    (travel,) = call(
        add_kernel, [((16, BRANCH + PART, C), BF)], [], (out, keep, partner), "add_cores", 1_000_000, 8
    )
    travel = lax.all_to_all(travel, "chan", split_axis=0, concat_axis=0, tiled=True)

    sent = jnp.sum(travel[:, BRANCH:].astype(F32), axis=0).astype(BF)
    sent = jnp.concatenate([sent, extra], axis=0)
    got = lax.ppermute(sent, "region", cube_pairs(count, 1))
    output, grad, kernel_part = call(
        taps_kernel,
        [((ROWS, PIX), BF), ((ROWS, PIX), BF), ((8, C), BF)],
        [((ROWS, 2 * PIX), F32), square, ((3, 64, 128), F32), padded],
        (travel, x, pad_x),
        "kernel_taps",
        400_000_000,
        16,
    )
    step = [((LONG + 8, C), BF)]
    (sent,) = call(first_step_kernel, step, [], (sent, got, kernel_part), "step", 100_000, 4)
    got = lax.ppermute(sent, "region", cube_pairs(count, 2))
    (sent,) = call(next_step_kernel, step, [], (sent, got), "step", 100_000, 4)
    got = lax.ppermute(sent, "region", cube_pairs(count, 4))
    mine, kernel_part = call(
        spread_kernel, [((peers, LONG, C), BF), ((8, 192), F32)],
        [((LONG, C), BF), ((16,), None)], (sent, got), "spread", 1_000_000, 8, far=(2,),
    )
    mine = lax.all_to_all(mine, "chan", split_axis=0, concat_axis=0, tiled=True)

    grad_near, grad_far = both_sides(grad)
    kernel_part = sum_four(kernel_part, swap, cube_pairs(count, 1), cube_pairs(count, 1, 1))
    (input_grad,) = call(
        functools.partial(backward_kernel, total_tiles),
        [block],
        [padded, square, taps, ((ROWS, 1024), BF)],
        (region, neighbours, grad, grad_near, grad_far, kernel, upstream),
        "backward_conv",
        400_000_000,
        16,
        smem=(0,),
    )

    mine, kernel_part, input_grad = lax.optimization_barrier((mine, kernel_part, input_grad))
    other = lax.ppermute(mine, "region", swap)
    kernel_part = kernel_part.reshape(8, 3, 64).transpose(1, 0, 2).reshape(CH, 64)
    kernel_part = kernel_part[:, :49] * factor
    grads = [((HID, C), F32), ((C, HID), F32)]
    scratch = [((768, C), F32), ((C, 768), F32), ((12,), None)]
    placed = call(
        functools.partial(place_own_kernel, factor),
        grads, scratch, (region, mine), "place_own", 1_000_000, 16, smem=(0,), far=(2, 3),
    )
    own_extra = mine[0, PART:].astype(F32)
    for j in range(1, peers):
        own_extra = own_extra + mine[j, PART:].astype(F32)
    vectors = [((HID,), F32)] + [((C,), F32)] * 3
    grad_weight_in, grad_weight_out, grad_bias, grad_gain, grad_shift, grad_scale = call(
        functools.partial(place_other_kernel, factor),
        grads + vectors,
        scratch[:2] + vectors + [((16,), None)],
        (region, other, *placed, own_extra), "place_other", 1_000_000, 16,
        smem=(0,), far=(2, 3, 5, 6, 7, 8, 9, 10), aliases={2: 0, 3: 1},
    )
    return (
        output.reshape(features.shape),
        input_grad.reshape(features.shape),
        grad_weight_in,
        grad_weight_out,
        grad_bias,
        grad_gain,
        grad_shift,
        grad_scale,
        kernel_part,
    )


def solution(mesh):
    block = P("chan", "region", None)
    in_specs = (block, block, P(None, "region"), P("chan", None)) + (P(),) * 6
    out_specs = (block, block) + (P(),) * 6 + (P("chan", None),)
    return jax.shard_map(
        per_device, mesh=mesh, in_specs=in_specs, out_specs=out_specs, check_vma=False
    )
```

```python
import functools
import math

import jax
import jax.numpy as jnp
from jax import lax
from jax.experimental import pallas as pl
from jax.experimental.pallas import tpu as pltpu
from jax.sharding import PartitionSpec as P

TS = 16
CH = 24
TILE = 16
PIX = 256
ROWS = CH * TILE
C = 384
HID = 1536
PART = 96
EXTRA = 8
LONG = PART + EXTRA
BRANCH = 32
F32 = jnp.float32
BF = jnp.bfloat16
NT = (((1,), (1,)), ((), ()))
NN = (((1,), (0,)), ((), ()))
TN = (((0,), (0,)), ((), ()))


def iota(shape, dim):
    return lax.broadcasted_iota(jnp.int32, shape, dim)


def dot(left, right, dims=NN):
    return lax.dot_general(left, right, dims, preferred_element_type=F32)


def eye(n):
    return (iota((n, n), 0) == iota((n, n), 1)).astype(F32).astype(BF)


def tile_major():
    column = iota((ROWS, ROWS), 1)
    target = (column & 15) * CH + (column >> 4)
    return (iota((ROWS, ROWS), 0) == target).astype(F32).astype(BF)


def chan_major():
    row = iota((ROWS, ROWS), 0)
    target = (row & 15) * CH + (row >> 4)
    return (iota((ROWS, ROWS), 1) == target).astype(F32).astype(BF)


def one_hots(lookup):
    row = iota((ROWS, 128), 0)
    lane = iota((ROWS, 128), 1)
    key = jnp.where(((row >> 4) & 7) == (lane >> 4), (row >> 7) * 16 + (row & 15), -1)
    parts = [
        (key == lookup[d : d + 1, :]).astype(F32).astype(BF) for d in (0, 4, 5, 1, 6, 7, 2, 3)
    ]
    return jnp.concatenate(parts, axis=1)


def fill_padded(pad, own, low, high, picks):
    apart = jnp.concatenate([picks[0:128, :], picks[256:384, :]], axis=0)
    for g in range(3):
        lanes = slice(g * 128, (g + 1) * 128)
        mine = own[:, lanes]
        sides = jnp.concatenate([low[lanes, :], high[lanes, :]], axis=0)

        def take(span, first, last):
            spread = dot(sides[:, span], apart[:, first:last], TN)
            return spread + dot(mine[span], picks[128:256, first:last])

        top = take(slice(128, 256), 0, 384)[80:128]
        bottom = take(slice(0, 128), 384, 768)[0:48]
        side = take(slice(0, 256), 768, 1024)
        pad[g, 3:19, 3:19, :] = own[:, lanes].astype(F32).reshape(16, 16, 128)
        pad[g, 0:3, 3:19, :] = top[:, 0:128].reshape(3, 16, 128)
        pad[g, 0:3, 0:3, :] = top[:, 128:256].reshape(3, 16, 128)[:, 13:16]
        pad[g, 0:3, 19:22, :] = top[:, 256:384].reshape(3, 16, 128)[:, 0:3]
        pad[g, 19:22, 3:19, :] = bottom[:, 0:128].reshape(3, 16, 128)
        pad[g, 19:22, 0:3, :] = bottom[:, 128:256].reshape(3, 16, 128)[:, 13:16]
        pad[g, 19:22, 19:22, :] = bottom[:, 256:384].reshape(3, 16, 128)[:, 0:3]
        pad[g, 3:19, 0:3, :] = side[:, 0:128].reshape(16, 16, 128)[:, 13:16]
        pad[g, 3:19, 19:22, :] = side[:, 128:256].reshape(16, 16, 128)[:, 0:3]


def lookup_rows(region, tables, total):
    raw = tables[CH:, 0:TILE].astype(jnp.int32)
    place = jnp.where(raw >= total, 3 * TILE, raw - (region[0] - 1) * TILE)
    repeat = ((iota((TILE, 128), 1) & 15) == iota((TILE, 128), 0)).astype(F32)
    return dot(place.astype(F32), repeat).astype(jnp.int32)


def spread_taps(kernel, weights):
    member = (iota((CH, ROWS), 0) == (iota((CH, ROWS), 1) >> 4)).astype(F32)
    wide = lax.dot_general(
        kernel, member, TN, preferred_element_type=F32, precision=lax.Precision.HIGHEST
    )
    for g in range(3):
        weights[g] = wide[:, g * 128 : (g + 1) * 128]


def convolve(pad, weights, result, flip):
    def group(g):
        for half in range(2):
            total = [None] * TS
            for b in range(7):
                taps = [
                    weights[g, pl.ds((48 - 7 * a - b) if flip else (7 * a + b), 1), :]
                    for a in range(7)
                ]
                taps = [jnp.broadcast_to(t, (8, 128)) for t in taps]
                for r in range(22):
                    value = pad[g, r, pl.ds(b + 8 * half, 8), :]
                    for a in range(7):
                        i = r - a
                        if 0 <= i < TS:
                            term = taps[a] * value
                            total[i] = term if total[i] is None else total[i] + term
            for i in range(TS):
                result[g, i, pl.ds(8 * half, 8), :] = total[i]

    for g in range(3):
        group(g)


def rows_of(result):
    return jnp.concatenate([result[g].reshape(PIX, 128) for g in range(3)], axis=1)


def prepare_kernel(
    total, region, tables, own, cotangent, own_t, upstream, weights, picks, order
):
    spread_taps(tables[0:CH, 0:49], weights)
    picks[...] = one_hots(lookup_rows(region, tables, total))
    order[...] = tile_major()
    own_t[...] = dot(eye(PIX), own[...], NT).astype(BF)
    upstream[...] = dot(order[...], cotangent[...]).astype(BF)


def sides_of(region, near, far):
    first = region[0] & 1 == 0
    low = jnp.where(first, far[...], near[...])
    high = jnp.where(first, near[...], far[...])
    return low, high


def forward_kernel(
    region, near, far, own_t, upstream, weights, picks, order, both, pad_out,
    pad, result, conv, sems,
):
    stores = [pltpu.make_async_copy(upstream, both.at[:, pl.ds(PIX, PIX)], sems.at[0])]
    stores[0].start()
    fill_padded(pad, own_t[...], *sides_of(region, near, far), picks)
    pad_out[...] = pad[...].astype(BF)
    convolve(pad, weights, result, False)
    conv[...] = dot(order[...], rows_of(result).astype(BF), NT).astype(BF)
    stores.append(pltpu.make_async_copy(conv, both.at[:, pl.ds(0, PIX)], sems.at[1]))
    stores[1].start()
    for store in stores:
        store.wait()


def taps_kernel(
    received, pad_x, branch, grad, kernel_grad, unpacked, gradient, sums, pad
):
    for t in range(TILE):
        part = received[t, 0:BRANCH, :].astype(F32)
        rows = slice(t * CH, (t + 1) * CH)
        unpacked[rows, 0:384] = part[0:CH]
        for i in range(3):
            piece = part[CH:, i * 128 : (i + 1) * 128]
            unpacked[t * CH + 8 * i : t * CH + 8 * (i + 1), 384:512] = piece
    both = dot(chan_major(), unpacked[...].astype(BF))
    branch[...] = both[:, :PIX].astype(BF)
    own_grad = both[:, PIX:].astype(BF)
    grad[...] = own_grad
    own = dot(eye(PIX), own_grad, NT)
    for g in range(3):
        gradient[g] = own[:, g * 128 : (g + 1) * 128].reshape(TS, TS, 128)
    sums[...] = jnp.zeros_like(sums)
    pad[...] = pad_x[...].astype(F32)

    def group(g):
        for b in range(7):
            total = [None] * 7
            for half in range(2):
                grads = [gradient[g, i, pl.ds(8 * half, 8), :] for i in range(TS)]
                for r in range(22):
                    value = pad[g, r, pl.ds(b + 8 * half, 8), :]
                    for a in range(7):
                        i = r - a
                        if 0 <= i < TS:
                            term = grads[i] * value
                            total[a] = term if total[a] is None else total[a] + term
            for a in range(7):
                sums[g, pl.ds(7 * a + b, 1), :] = jnp.sum(total[a], axis=0, keepdims=True)

    for g in range(3):
        group(g)
    spread = jnp.concatenate([sums[g] for g in range(3)], axis=1)
    member = (iota((32, ROWS), 0) == (iota((32, ROWS), 1) >> 4)).astype(F32)
    total = lax.dot_general(
        member, spread, NT, preferred_element_type=F32, precision=lax.Precision.HIGHEST
    )
    kernel_grad[...] = halves_of(jnp.concatenate([total[8 * i : 8 * i + 8] for i in range(3)], axis=1))


def halves_of(value):
    high = value.astype(BF).astype(F32)
    return jnp.concatenate([high, value - high], axis=1).astype(BF)


def backward_kernel(
    total, region, tables, own, near, far, cotangent, features, branch,
    input_grad, output, pad, result, weights, picks,
):
    output[...] = (features[...].astype(F32) + branch[...].astype(F32)).astype(BF)
    spread_taps(tables[0:CH, 0:49], weights)
    picks[...] = one_hots(lookup_rows(region, tables, total))
    own_t = dot(eye(PIX), own[...], NT).astype(BF)
    fill_padded(pad, own_t, *sides_of(region, near, far), picks)
    convolve(pad, weights, result, True)
    upstream = dot(eye(PIX), cotangent[...], NT)
    total = (upstream + rows_of(result)).astype(BF)
    input_grad[...] = dot(eye(ROWS), total, NT).astype(BF)


def normalize(columns):
    values = columns[:, :PIX].astype(F32)
    centered = values - jnp.mean(values, axis=0, keepdims=True)
    inv_std = lax.rsqrt(jnp.mean(centered * centered, axis=0, keepdims=True) + 1e-06)
    return centered * inv_std, inv_std


def stage_kernel(weight_in, weight_out, both):
    both[0:HID, :] = weight_in[...]
    for q in range(4):
        both[HID + q * C : HID + (q + 1) * C, :] = weight_out[:, q * C : (q + 1) * C]


def hidden_blocks(
    side, table, inputs, grad_mixed, bias, matrices, parts, mixed_out, grad_inputs, small,
):
    lane = iota((C, 128), 1)
    for q in range(4):
        bias[q * C : (q + 1) * C, :] = table[:, q : q + 1]
    for k in range(2):
        block = 2 * side + k
        rows = pl.ds(pl.multiple_of(block * C, C), C)
        weight_in = matrices[rows, :]
        weight_out = matrices[pl.ds(pl.multiple_of(HID + block * C, C), C), :]
        hidden = dot(weight_in, inputs) + bias[rows, :]
        cdf = 0.5 + 0.5 * lax.erf(hidden * 0.7071067811865476)
        activation = (hidden * cdf).astype(BF)
        slope = cdf + hidden * jnp.exp(-0.5 * hidden * hidden) * 0.3989422804014327
        mixed_out = mixed_out + dot(weight_out, activation)
        grad_hidden = dot(weight_out, grad_mixed, TN) * slope
        small = small + jnp.where(
            lane == block, jnp.sum(grad_hidden, axis=1, keepdims=True), 0.0
        )
        hidden_grad = grad_hidden.astype(BF)
        grad_inputs = grad_inputs + dot(weight_in, hidden_grad, TN)
        part = dot(hidden_grad, inputs, NT).astype(BF)
        for s in range(4):
            parts[4 * k + s] = part[s * PART : (s + 1) * PART]
        part = dot(grad_mixed, activation, NT).astype(BF)
        for s in range(4):
            parts[8 + 4 * k + s] = part[s * PART : (s + 1) * PART]
    return mixed_out, grad_inputs, small


def first_half_kernel(
    region, columns, vectors, matrices,
    parts, mixed_sum, grad_sum, small_sum, inputs_ref, mixed_ref, bias,
):
    table = jnp.transpose(vectors[...])
    normed, _ = normalize(columns)
    inputs = (normed * table[:, 4:5] + table[:, 5:6]).astype(BF)
    grad_mixed = (table[:, 6:7] * columns[:, PIX:].astype(F32)).astype(BF)
    inputs_ref[...] = inputs
    mixed_ref[...] = grad_mixed
    zeros = jnp.zeros((C, PIX), F32)
    mixed_sum[...], grad_sum[...], small_sum[...] = hidden_blocks(
        1 - (region[0] & 1), table, inputs, grad_mixed, bias,
        matrices, parts, zeros, zeros, jnp.zeros((C, 128), F32),
    )


def second_half_kernel(
    region, columns, vectors, matrices,
    mixed_sum, grad_sum, small_sum, inputs, grad_mixed, out, parts, extra, bias,
):
    table = jnp.transpose(vectors[...])
    gain = table[:, 4:5]
    scale = table[:, 6:7]
    mixed_out, grad_inputs, small = hidden_blocks(
        region[0] & 1, table, inputs[...], grad_mixed[...], bias,
        matrices, parts, mixed_sum[...], grad_sum[...], small_sum[...],
    )
    normed, inv_std = normalize(columns)
    upstream = columns[:, PIX:].astype(F32)
    branch = scale * mixed_out
    grad_scale = jnp.sum(upstream * mixed_out, axis=1, keepdims=True)
    grad_gain = jnp.sum(grad_inputs * normed, axis=1, keepdims=True)
    grad_shift = jnp.sum(grad_inputs, axis=1, keepdims=True)
    grad_normed = grad_inputs * gain
    grad_conv = (
        grad_normed
        - jnp.mean(grad_normed, axis=0, keepdims=True)
        - normed * jnp.mean(grad_normed * normed, axis=0, keepdims=True)
    ) * inv_std
    for j in range(16):
        rows = slice(j * CH, (j + 1) * CH)
        side = grad_conv[rows, 128:]
        first = jnp.concatenate([branch[rows], grad_conv[rows, :128]], axis=1)
        last = jnp.concatenate([side[8 * i : 8 * i + 8] for i in range(3)], axis=1)
        out[j] = jnp.concatenate([first, last], axis=0).astype(BF)
    lane = iota((C, 128), 1)
    small = small + jnp.where(lane == 4, grad_gain, 0.0)
    small = small + jnp.where(lane == 5, grad_shift, 0.0)
    small = small + jnp.where(lane == 6, grad_scale, 0.0)
    extra[...] = jnp.transpose(small)[0:EXTRA].astype(BF)


def add_kernel(out, first, second, total):
    total[:, 0:BRANCH, :] = out[...]
    total[:, BRANCH:, :] = (first[...].astype(F32) + second[...].astype(F32)).astype(BF)


def first_step_kernel(sent, got, kernel_grad, total):
    total[0:LONG, :] = (sent[...].astype(F32) + got[...].astype(F32)).astype(BF)
    total[LONG:, :] = kernel_grad[...]


def joined(sent, got):
    value = sent[...].astype(F32) + got[...].astype(F32)
    return value[0:LONG].astype(BF), value[LONG:, :192] + value[LONG:, 192:]


def next_step_kernel(sent, got, total):
    weights, taps = joined(sent, got)
    total[0:LONG, :] = weights
    total[LONG:, :] = halves_of(taps)


def spread_kernel(sent, got, total, kernel_grad, value, sems):
    value[...], kernel_grad[...] = joined(sent, got)
    stores = [pltpu.make_async_copy(value, total.at[j], sems.at[j]) for j in range(16)]
    for store in stores:
        store.start()
    for store in stores:
        store.wait()


def place(factor, side, ref, grad_in, grad_out, tall, wide, sems):
    half = pl.multiple_of(side * 768, 768)
    stores = []
    for j in range(8):
        rows = pl.ds(j * PART, PART)
        tall[rows, :] = ref[j, 0:PART, :].astype(F32) * factor
        target = grad_in.at[pl.ds(half + j * PART, PART), :]
        stores.append(pltpu.make_async_copy(tall.at[rows, :], target, sems.at[j]))
        stores[-1].start()
    for s in range(4):
        rows = pl.ds(s * PART, PART)
        for k in range(2):
            wide[rows, k * C : (k + 1) * C] = ref[8 + 4 * k + s, 0:PART, :].astype(F32) * factor
        target = grad_out.at[rows, pl.ds(half, 768)]
        stores.append(pltpu.make_async_copy(wide.at[rows, :], target, sems.at[8 + s]))
        stores[-1].start()
    return stores


def place_own_kernel(factor, region, ref, grad_in, grad_out, tall, wide, sems):
    for store in place(factor, region[0] & 1, ref, grad_in, grad_out, tall, wide, sems):
        store.wait()


def place_other_kernel(
    factor, region, ref, in_a, out_a, own_extra, grad_in, grad_out, bias, gain, shift, scale,
    tall, wide, bias_ref, gain_ref, shift_ref, scale_ref, sems,
):
    stores = place(factor, 1 - (region[0] & 1), ref, grad_in, grad_out, tall, wide, sems)
    small = ref[0, PART:, :].astype(F32)
    for j in range(1, 16):
        small = small + ref[j, PART:, :].astype(F32)
    small = (own_extra[...] + small) * factor
    for q in range(4):
        bias_ref[q * C : (q + 1) * C] = small[q]
    gain_ref[...] = small[4]
    shift_ref[...] = small[5]
    scale_ref[...] = small[6]
    pairs = [(bias_ref, bias), (gain_ref, gain), (shift_ref, shift), (scale_ref, scale)]
    for i, pair in enumerate(pairs):
        stores.append(pltpu.make_async_copy(*pair, sems.at[12 + i]))
        stores[-1].start()
    for store in stores:
        store.wait()


def call(
    body, shapes, scratch, args, name, flops, limit, smem=(), far=(), anywhere=(), aliases=None
):
    spaces = [pltpu.VMEM] * (len(args) + len(shapes))
    for space, places in ((pltpu.SMEM, smem), (pltpu.HBM, far), (pl.ANY, anywhere)):
        for i in places:
            spaces[i] = space
    spaces = [pl.BlockSpec(memory_space=space) for space in spaces]
    moved = sum(a.size * a.dtype.itemsize for a in args)
    moved += sum(math.prod(s) * jnp.dtype(d).itemsize for s, d in shapes)
    return pl.pallas_call(
        body,
        out_shape=[jax.ShapeDtypeStruct(s, d) for s, d in shapes],
        in_specs=spaces[: len(args)],
        out_specs=spaces[len(args) :],
        scratch_shapes=[
            pltpu.SemaphoreType.DMA(s) if d is None else pltpu.VMEM(s, d) for s, d in scratch
        ],
        compiler_params=pltpu.CompilerParams(vmem_limit_bytes=int(limit * 1024 * 1024)),
        cost_estimate=pl.CostEstimate(flops=flops, bytes_accessed=moved, transcendentals=0),
        input_output_aliases=aliases or {},
        name=name,
    )(*args)


def both_sides(field):
    count = lax.axis_size("region")
    near = [(i, i ^ 1) for i in range(count)]
    far = [(i, ((i + 1) ^ 1) - 1) for i in range(1, count - 1)]
    across = lax.ppermute(field, "region", far)
    return lax.ppermute(field, "region", near), across


def cube_pairs(count, bit, core=0):
    ring = count // 2
    label = [z ^ (z >> 1) for z in range(ring)]
    place = {g: z for z, g in enumerate(label)}
    return [
        (2 * z + c, 2 * place[label[z] ^ bit] + (c ^ core)) for z in range(ring) for c in range(2)
    ]


def sum_four(value, first, second, both):
    near, far, across = (lax.ppermute(value, "region", pairs) for pairs in (first, second, both))
    return (value + near) + (far + across)


def per_device(
    features, cotangent, neighbours, kernel, norm_gain, norm_shift,
    weight_in, bias_in, weight_out, layer_scale,
):
    count = lax.axis_size("region")
    peers = lax.axis_size("chan")
    region = lax.axis_index("region").astype(jnp.int32).reshape(1)
    total_tiles = TILE * count
    factor = 1.0 / math.sqrt(total_tiles * PIX)
    swap = [(i, i ^ 1) for i in range(count)]

    x = features.reshape(ROWS, PIX)
    upstream = cotangent.reshape(ROWS, PIX)
    x_near, x_far = both_sides(x)
    vectors = jnp.concatenate(
        [
            bias_in.reshape(4, C), norm_gain[None], norm_shift[None], layer_scale[None],
            jnp.zeros((1, C), F32),
        ],
        axis=0,
    )

    padded = ((3, 22, 24, 128), F32)
    square = ((3, 16, 16, 128), F32)
    taps = ((3, 49, 128), F32)
    block = ((ROWS, PIX), BF)
    tables = jnp.pad(kernel, ((0, 8), (0, 0))) + jnp.pad(
        neighbours, ((CH, 0), (0, 49 - TILE))
    ).astype(F32)
    ready = call(
        functools.partial(prepare_kernel, total_tiles),
        [((PIX, ROWS), BF), block, taps, ((ROWS, 1024), BF), ((ROWS, ROWS), BF)],
        [],
        (region, tables, x, upstream),
        "prepare",
        200_000_000,
        16,
        smem=(0,),
    )
    columns, pad_x = call(
        forward_kernel,
        [((ROWS, 2 * PIX), BF), (padded[0], BF)],
        [padded, square, block, ((2,), None)],
        (region, x_near, x_far, *ready),
        "forward_conv",
        400_000_000,
        16,
        smem=(0,),
        far=(8,),
    )
    columns = lax.all_to_all(columns, "chan", split_axis=0, concat_axis=0, tiled=True)

    staged = call(
        stage_kernel, [((2 * HID, C), BF)], [], (weight_in, weight_out),
        "stage", 1_000_000, 8,
    )
    halves = (16, PART, C)
    pixels = (region, columns, vectors, *staged)
    scratch = [((HID, 1), F32)]
    sums = [((C, PIX), F32), ((C, PIX), F32), ((C, 128), F32), ((C, PIX), BF), ((C, PIX), BF)]
    send, *partial = call(
        first_half_kernel,
        [(halves, BF)] + sums,
        scratch,
        pixels,
        "pixels_first",
        1_000_000_000,
        24,
        smem=(0,),
    )
    partner = lax.ppermute(send, "region", swap)
    out, keep, extra = call(
        second_half_kernel,
        [((16, BRANCH, C), BF), (halves, BF), ((EXTRA, C), BF)],
        scratch,
        (*pixels, *partial),
        "pixels_second",
        1_000_000_000,
        24,
        smem=(0,),
    )
    (travel,) = call(
        add_kernel, [((16, BRANCH + PART, C), BF)], [], (out, keep, partner), "add_cores", 1_000_000, 8
    )
    travel = lax.all_to_all(travel, "chan", split_axis=0, concat_axis=0, tiled=True)

    sent = jnp.sum(travel[:, BRANCH:].astype(F32), axis=0).astype(BF)
    sent = jnp.concatenate([sent, extra], axis=0)
    got = lax.ppermute(sent, "region", cube_pairs(count, 1))
    branch, grad, kernel_part = call(
        taps_kernel,
        [((ROWS, PIX), BF), ((ROWS, PIX), BF), ((8, C), BF)],
        [((ROWS, 2 * PIX), F32), square, ((3, 64, 128), F32), padded],
        (travel, pad_x),
        "kernel_taps",
        400_000_000,
        16,
    )
    step = [((LONG + 8, C), BF)]
    (sent,) = call(first_step_kernel, step, [], (sent, got, kernel_part), "step", 100_000, 4)
    got = lax.ppermute(sent, "region", cube_pairs(count, 2))
    (sent,) = call(next_step_kernel, step, [], (sent, got), "step", 100_000, 4)
    got = lax.ppermute(sent, "region", cube_pairs(count, 4))
    mine, kernel_part = call(
        spread_kernel, [((peers, LONG, C), BF), ((8, 192), F32)],
        [((LONG, C), BF), ((16,), None)], (sent, got), "spread", 1_000_000, 8, far=(2,),
    )
    mine = lax.all_to_all(mine, "chan", split_axis=0, concat_axis=0, tiled=True)

    grad_near, grad_far = both_sides(grad)
    kernel_part = sum_four(kernel_part, swap, cube_pairs(count, 1), cube_pairs(count, 1, 1))
    input_grad, output = call(
        functools.partial(backward_kernel, total_tiles),
        [block, block],
        [padded, square, taps, ((ROWS, 1024), BF)],
        (region, tables, grad, grad_near, grad_far, upstream, x, branch),
        "backward_conv",
        400_000_000,
        16,
        smem=(0,),
    )

    mine, kernel_part, input_grad = lax.optimization_barrier((mine, kernel_part, input_grad))
    other = lax.ppermute(mine, "region", swap)
    kernel_part = kernel_part.reshape(8, 3, 64).transpose(1, 0, 2).reshape(CH, 64)
    kernel_part = kernel_part[:, :49] * factor
    grads = [((HID, C), F32), ((C, HID), F32)]
    scratch = [((768, C), F32), ((C, 768), F32), ((12,), None)]
    placed = call(
        functools.partial(place_own_kernel, factor),
        grads, scratch, (region, mine), "place_own", 1_000_000, 16, smem=(0,), far=(2, 3),
    )
    own_extra = mine[0, PART:].astype(F32)
    for j in range(1, peers):
        own_extra = own_extra + mine[j, PART:].astype(F32)
    vectors = [((HID,), F32)] + [((C,), F32)] * 3
    grad_weight_in, grad_weight_out, grad_bias, grad_gain, grad_shift, grad_scale = call(
        functools.partial(place_other_kernel, factor),
        grads + vectors,
        scratch[:2] + vectors + [((16,), None)],
        (region, other, *placed, own_extra), "place_other", 1_000_000, 16,
        smem=(0,), far=(2, 3, 5, 6, 7, 8, 9, 10), aliases={2: 0, 3: 1},
    )
    return (
        output.reshape(features.shape),
        input_grad.reshape(features.shape),
        grad_weight_in,
        grad_weight_out,
        grad_bias,
        grad_gain,
        grad_shift,
        grad_scale,
        kernel_part,
    )


def solution(mesh):
    block = P("chan", "region", None)
    in_specs = (block, block, P(None, "region"), P("chan", None)) + (P(),) * 6
    out_specs = (block, block) + (P(),) * 6 + (P("chan", None),)
    return jax.shard_map(
        per_device, mesh=mesh, in_specs=in_specs, out_specs=out_specs, check_vma=False
    )
```
